512 devices in a mesh: row: 32 (over y, x), col: 16 (over z, core).
Axes of the slice: x: 4, y: 8, z: 8, core: 2. Of those that a mesh axis runs over, the one named last changes fastest.
Arguments:
- sequence_features: bfloat16 [128, 1024, 64], P(None, ('row', 'col')), may hold values from -6 to 6
- standardize_scale: float32 [64], replicated, may hold values from 0.1 to 1.9
- standardize_shift: float32 [64], replicated, may hold values from -3 to 3
- first_projection_kernel: bfloat16 [64, 32], replicated, may hold values from -0.75 to 0.75
- first_projection_shift: float32 [32], replicated, may hold values from -3 to 3
- second_projection_kernel: bfloat16 [64, 32], replicated, may hold values from -0.75 to 0.75
- second_projection_shift: float32 [32], replicated, may hold values from -3 to 3
- final_projection_kernel: bfloat16 [1024, 128], replicated, may hold values from -2 to 2
- final_projection_shift: float32 [128], replicated, may hold values from -3 to 3
- cross_molecule_shift: float32 [128], replicated, may hold values from -3 to 3
- residue_molecule_label: int32 [1024], replicated, may hold values from 0 to 3, never falling along the last dimension, each value on 1 to 512 neighbouring positions
- selected_tile_couples: int32 [16, 2], replicated, may hold values from 0 to 7, as said below
- result_adjoint: bfloat16 [1024, 1024, 128], P('row', 'col'), may hold values from -6 to 6
Outputs:
- pair_out: bfloat16 [1024, 1024, 128], P('row', 'col')
- left_grad: float32 [128, 1024, 32], P(None, ('row', 'col'))
- right_grad: float32 [128, 1024, 32], P(None, ('col', 'row'))
The draws below stay inside these ranges and needn't reach their ends.
Inputs may be any that keep to these rules, and one draw needn't show every extreme that they name: `selected_tile_couples`: pairs are distinct; every diagonal pair (k, k) for k below 8 is listed. `residue_molecule_label`: never falls along the tokens.
All inputs are finite; a program needn't handle non-finite values.
Results may differ from the reference program's by a relative error of at most 0.0057.
Values may be sent and summed in bfloat16 or wider, within the bound.
A program may use at most 64 MiB of HBM per device.

```python
import math
import jax
import jax.numpy as jnp
import numpy as np
from jax import lax

SEQUENCE_TOTAL = 128
FEATURE_DEPTH = 64
PROJ_DIM = 32
P_SIZE = 128
BLK = 128
CHAINS = 4
RESIDUE_TOTAL = 1024
NB = 8
NLIST = 16


def draw_selected_tile_couples(key, part):
    key = jax.random.fold_in(key, 7)
    first, second = jax.random.split(key, 2)
    diagonal = jnp.arange(NB, dtype=jnp.int32)
    others = jax.random.permutation(first, NB * (NB - 1))[:NLIST - NB].astype(jnp.int32)
    span = max(NB - 1, 1)
    other_rows = others // span
    raw_cols = others % span
    other_cols = raw_cols + (raw_cols >= other_rows).astype(jnp.int32)
    rows_all = jnp.concatenate([diagonal, other_rows])
    cols_all = jnp.concatenate([diagonal, other_cols])
    order = jax.random.permutation(second, NLIST)
    return jnp.stack([rows_all[order], cols_all[order]], axis=1).astype(jnp.int32)


def block_levels(key, shape, cuts, least, high):
    level = 1.0
    for position, shards_of in cuts:
        draws = jax.random.uniform(jax.random.fold_in(jax.random.fold_in(key, 6), position), (shards_of,), jnp.float32, least / len(cuts), high / len(cuts))
        level = level * jnp.repeat(jnp.exp(draws), shape[position] // shards_of).reshape((-1,) + (1,) * (len(shape) - 1 - position))
    return level


def profile(number_of, total, most, skew):
    portions = [(1 << 20) // math.isqrt(rank ** skew) + 1 for rank in range(2, number_of + 1)]
    spare, counts = total - most - (number_of - 1), [1] * (number_of - 1)
    while spare > 0:
        candidates = [i for i in range(number_of - 1) if counts[i] < most]
        pool, remaining = sum([portions[i] for i in candidates]), spare
        for i in candidates:
            more = min(most - counts[i], max(1, remaining * portions[i] // pool), spare)
            counts[i] = counts[i] + more
            spare = spare - more
    return np.array([most] + counts)


def uneven_parts(rng, count, total, limit, slope):
    if count == 2:
        one = jax.random.randint(rng, (), max(1, total - limit), min(limit, total - 1) + 1)
        return jnp.stack([one, total - one])
    lengths = jnp.asarray(profile(count, total, limit, slope), jnp.int32)
    pairs = (count - 1) // 2
    source_of, receiver = lengths[1:1 + 2 * pairs:2], lengths[2:2 + 2 * pairs:2]
    slack = jnp.minimum(source_of - 1, limit - receiver)
    shifted = jax.random.randint(jax.random.fold_in(rng, 1), (pairs,), 0, 1 << 20) % (slack + 1)
    lengths = lengths.at[1:1 + 2 * pairs:2].set(source_of - shifted).at[2:2 + 2 * pairs:2].set(receiver + shifted)
    return lengths[jax.random.permutation(jax.random.fold_in(rng, 2), count)]


def bell_draw(stream_key, shape, deviation, reach, cuts=(), kind=jnp.bfloat16):
    array = deviation * jax.random.normal(stream_key, shape, jnp.float32)
    if cuts:
        array = array * block_levels(stream_key, shape, cuts, -0.22, 0.18)
    return jnp.clip(array, -reach, reach).astype(kind)


def setup_inputs(seed: int = 0) -> dict:
    arg_keys = jax.random.split(jax.random.key(seed), 14)
    return {
        "sequence_features": bell_draw(arg_keys[0], (SEQUENCE_TOTAL, RESIDUE_TOTAL, FEATURE_DEPTH), 1.0, 6.0, ((1, 512),)),
        "standardize_scale": jnp.clip(1.0 + 0.18 * jax.random.normal(arg_keys[1], (FEATURE_DEPTH,), jnp.float32), 0.1, 1.9),
        "standardize_shift": bell_draw(arg_keys[2], (FEATURE_DEPTH,), 0.5, 3.0, (), jnp.float32),
        "first_projection_kernel": bell_draw(arg_keys[3], (FEATURE_DEPTH, PROJ_DIM), FEATURE_DEPTH ** -0.5, 0.75),
        "first_projection_shift": bell_draw(arg_keys[4], (PROJ_DIM,), 0.5, 3.0, (), jnp.float32),
        "second_projection_kernel": bell_draw(arg_keys[5], (FEATURE_DEPTH, PROJ_DIM), FEATURE_DEPTH ** -0.5, 0.75),
        "second_projection_shift": bell_draw(arg_keys[6], (PROJ_DIM,), 0.5, 3.0, (), jnp.float32),
        "final_projection_kernel": bell_draw(arg_keys[7], (PROJ_DIM * PROJ_DIM, P_SIZE), (PROJ_DIM * PROJ_DIM // SEQUENCE_TOTAL) ** -0.5, 2.0),
        "final_projection_shift": bell_draw(arg_keys[8], (P_SIZE,), 0.5, 3.0, (), jnp.float32),
        "cross_molecule_shift": bell_draw(arg_keys[9], (P_SIZE,), 0.5, 3.0, (), jnp.float32),
        "residue_molecule_label": jnp.searchsorted(jnp.cumsum(uneven_parts(arg_keys[10], CHAINS, RESIDUE_TOTAL, RESIDUE_TOTAL // 2, 0)), jnp.arange(RESIDUE_TOTAL), side="right").astype(jnp.int32),
        "selected_tile_couples": draw_selected_tile_couples(jax.random.fold_in(arg_keys[13], 71), 0),
        "result_adjoint": bell_draw(arg_keys[12], (RESIDUE_TOTAL, RESIDUE_TOTAL, P_SIZE), 1.0, 6.0, ((0, 32), (1, 16))),
    }


def standardize_features(sequence_features, standardize_scale, standardize_shift):
    result_entries = sequence_features.astype(jnp.float32)
    mean = lax.optimization_barrier(jnp.mean(result_entries, axis=-1, keepdims=True))
    var = lax.optimization_barrier(jnp.mean((result_entries - mean) ** 2, axis=-1, keepdims=True))
    return ((result_entries - mean) * lax.rsqrt(var + 1e-05) * standardize_scale + standardize_shift).astype(jnp.bfloat16)

def project(standardized_features, weight, bias):
    mixed = jnp.einsum('slc,cf->slf', standardized_features.astype(jnp.float32), weight.astype(jnp.float32))
    return (mixed + bias).astype(jnp.bfloat16)

def reference(sequence_features, standardize_scale, standardize_shift, first_projection_kernel, first_projection_shift, second_projection_kernel, second_projection_shift, final_projection_kernel, final_projection_shift, cross_molecule_shift, residue_molecule_label, selected_tile_couples, result_adjoint):
    standardized_features = standardize_features(sequence_features, standardize_scale, standardize_shift)
    left = project(standardized_features, first_projection_kernel, first_projection_shift)
    right = project(standardized_features, second_projection_kernel, second_projection_shift)
    zero = jnp.zeros((), jnp.int32)

    def one_block(carry, pair):
        pair_out, left_grad, right_grad = carry
        rows = (pair[0] * BLK).astype(jnp.int32)
        cols = (pair[1] * BLK).astype(jnp.int32)
        left_blk = lax.dynamic_slice(left, (zero, rows, zero), (SEQUENCE_TOTAL, BLK, PROJ_DIM))
        right_blk = lax.dynamic_slice(right, (zero, cols, zero), (SEQUENCE_TOTAL, BLK, PROJ_DIM))
        outer = jnp.einsum('sic,sje->ijce', left_blk.astype(jnp.float32), right_blk.astype(jnp.float32)) / SEQUENCE_TOTAL
        outer = outer.astype(jnp.bfloat16).reshape(BLK * BLK, PROJ_DIM * PROJ_DIM)
        chain_rows = lax.dynamic_slice(residue_molecule_label, (rows,), (BLK,))
        chain_cols = lax.dynamic_slice(residue_molecule_label, (cols,), (BLK,))
        apart = (chain_rows[:, None] != chain_cols[None, :]).astype(jnp.float32)
        value = jnp.dot(outer, final_projection_kernel, preferred_element_type=jnp.float32).reshape(BLK, BLK, P_SIZE)
        value = (value + final_projection_shift + cross_molecule_shift * apart[:, :, None]).astype(jnp.bfloat16)
        pair_out = lax.dynamic_update_slice(pair_out, value, (rows, cols, zero))
        cotangent = lax.dynamic_slice(result_adjoint, (rows, cols, zero), (BLK, BLK, P_SIZE)).reshape(BLK * BLK, P_SIZE)
        outer_grad = jnp.dot(cotangent, final_projection_kernel.T, preferred_element_type=jnp.float32)
        outer_grad = outer_grad.astype(jnp.bfloat16).reshape(BLK, BLK, PROJ_DIM, PROJ_DIM).astype(jnp.float32)
        delta_left = jnp.einsum('ijce,sje->sic', outer_grad, right_blk.astype(jnp.float32)) / SEQUENCE_TOTAL
        delta_right = jnp.einsum('ijce,sic->sje', outer_grad, left_blk.astype(jnp.float32)) / SEQUENCE_TOTAL
        old_left = lax.dynamic_slice(left_grad, (zero, rows, zero), (SEQUENCE_TOTAL, BLK, PROJ_DIM))
        left_grad = lax.dynamic_update_slice(left_grad, old_left + delta_left, (zero, rows, zero))
        old_right = lax.dynamic_slice(right_grad, (zero, cols, zero), (SEQUENCE_TOTAL, BLK, PROJ_DIM))
        right_grad = lax.dynamic_update_slice(right_grad, old_right + delta_right, (zero, cols, zero))
        return ((pair_out, left_grad, right_grad), None)
    start = (jnp.zeros((RESIDUE_TOTAL, RESIDUE_TOTAL, P_SIZE), jnp.bfloat16), jnp.zeros((SEQUENCE_TOTAL, RESIDUE_TOTAL, PROJ_DIM), jnp.float32), jnp.zeros((SEQUENCE_TOTAL, RESIDUE_TOTAL, PROJ_DIM), jnp.float32))
    (pair_out, left_grad, right_grad), unused = lax.scan(one_block, start, selected_tile_couples)
    return (pair_out, left_grad, right_grad)
```

```python
import jax
import jax.numpy as jnp
from jax import lax
from jax.experimental import pallas as pl
from jax.experimental.pallas import tpu as pltpu
from jax.sharding import PartitionSpec as P

F32 = jnp.float32
BF16 = jnp.bfloat16
MESH = pl.DeviceIdType.MESH

NX, NY, NZ, NK = 4, 8, 8, 2
NCOL = NZ * NK
S = 128
C = 32
PW = 128
TI = 32
TJ = 64
OWN = 2 * C
G = 4
NG = TI // G
BLK = 128


def place():
    row, col = lax.axis_index("row"), lax.axis_index("col")
    return row, col, row % NX, row // NX, col // NK, col % NK


def remote(src, dst, send, recv, row, col):
    return pltpu.make_async_remote_copy(
        src_ref=src, dst_ref=dst, send_sem=send, recv_sem=recv,
        device_id=(row, col), device_id_type=MESH,
    )


def down(vector, width):
    return jnp.broadcast_to(vector, (width, vector.shape[1])).T


def gather_kernel(
    x_ref, gain_ref, shift_ref, w1_ref, b1_ref, w2_ref, b2_ref,
    lt_ref, rt_ref,
    own, stage,
    l_send, l_fwd, l_recv, s_send, s_recv, r_send, r_recv,
):
    row, col, x, y, z, k = place()
    home = x // 2
    barrier = pltpu.get_barrier_semaphore()

    def greet(r, c):
        pl.semaphore_signal(barrier, inc=1, device_id=(r, c), device_id_type=MESH)

    for dz in range(1, NZ):
        greet(row, lax.rem(z + dz, NZ) * NK + k)
    greet(row, z * NK + 1 - k)
    for dz in range(1, NZ):
        greet(z * NX + x, lax.rem(z + dz, NZ) * NK + k)

    @pl.when(y != z)
    def _():
        greet(z * NX + x, z * NK + k)

    for xx in range(2):
        for kk in range(NK):
            @pl.when(jnp.logical_or(2 * k + xx != x, kk != k))
            def _(xx=xx, kk=kk):
                greet(y * NX + 2 * k + xx, z * NK + kk)

    gain = down(gain_ref[...], S)
    shift = down(shift_ref[...], S)
    b1 = down(b1_ref[...], S)
    b2 = down(b2_ref[...], S)
    for t in range(2):
        v = x_ref[t].astype(F32)
        mean = jnp.mean(v, axis=0, keepdims=True)
        var = jnp.mean((v - mean) ** 2, axis=0, keepdims=True)
        n = ((v - mean) * lax.rsqrt(var + 1e-05) * gain + shift).astype(BF16)
        own[0, t * C:(t + 1) * C, :] = (
            jnp.dot(w1_ref[...], n, preferred_element_type=F32) + b1
        ).astype(BF16)
        own[1, t * C:(t + 1) * C, :] = (
            jnp.dot(w2_ref[...], n, preferred_element_type=F32) + b2
        ).astype(BF16)

    many = 20 - (y == z).astype(jnp.int32) - (home == k).astype(jnp.int32)
    pl.semaphore_wait(barrier, many)

    def block(ref, index):
        return ref.at[pl.ds(pl.multiple_of(index * OWN, OWN), OWN), :]

    def leg1(dy):
        y2 = lax.rem(y + dy, NY)
        return remote(own.at[1], stage.at[z], s_send.at[dy], s_recv.at[z],
                      y2 * NX + x, y * NK + k)

    def left(dz):
        c2 = lax.rem(z + dz, NZ) * NK + k if dz else z * NK + 1 - k
        return remote(own.at[0], block(lt_ref, col), l_send.at[dz], l_recv.at[col], row, c2)

    for dy in range(1, NY):
        leg1(dy).start()

    @pl.when(y != z)
    def _():
        leg1(0).start()

    for dz in range(NZ):
        left(dz).start()

    @pl.when(y == z)
    def _():
        stage[z] = own[1]

    lt_ref[pl.ds(pl.multiple_of(col * OWN, OWN), OWN), :] = own[0]

    def leg2(d, dx):
        slot = lax.rem(y + d, NZ)
        b = (x % 2) * NCOL + slot * NK + k
        return remote(stage.at[slot], block(rt_ref, b), r_send.at[d, dx], r_recv.at[b],
                      y * NX + lax.rem(x + dx, NX), z * NK + home)

    def pass_on(dz):
        c2 = lax.rem(z + dz, NZ) * NK + k
        return remote(block(lt_ref, c2), block(lt_ref, c2), l_fwd.at[dz], l_recv.at[c2],
                      row, z * NK + 1 - k)

    def arrived(ref, sem):
        pltpu.make_async_copy(ref, ref, sem).wait()

    for d in (0, 1, 7, 2, 6, 3, 5, 4):
        slot = lax.rem(y + d, NZ)
        if d == 0:
            @pl.when(y != z)
            def _():
                arrived(stage.at[slot], s_recv.at[slot])
        else:
            arrived(stage.at[slot], s_recv.at[slot])
        for dx in range(1, NX):
            leg2(d, dx).start()

        @pl.when(home != k)
        def _():
            leg2(d, 0).start()

        @pl.when(home == k)
        def _():
            b = (x % 2) * NCOL + slot * NK + k
            rt_ref[pl.ds(pl.multiple_of(b * OWN, OWN), OWN), :] = stage[slot]

        if d:
            c2 = lax.rem(z + d, NZ) * NK + k
            arrived(block(lt_ref, c2), l_recv.at[c2])
            pass_on(d).start()

    for zz in range(NZ):
        c2 = zz * NK + 1 - k
        arrived(block(lt_ref, c2), l_recv.at[c2])
    for xx in range(2):
        for kk in range(NK):
            @pl.when(jnp.logical_or(2 * k + xx != x, kk != k))
            def _(xx=xx, kk=kk):
                for zz in range(NZ):
                    b = xx * NCOL + zz * NK + kk
                    arrived(block(rt_ref, b), r_recv.at[b])

    for d in range(NY):
        left(d).wait_send()
        if d:
            leg1(d).wait_send()
            pass_on(d).wait_send()
        for dx in range(1, NX):
            leg2(d, dx).wait_send()

    @pl.when(y != z)
    def _():
        leg1(0).wait_send()

    @pl.when(home != k)
    def _():
        for d in range(NY):
            leg2(d, 0).wait_send()


def tile_kernel(
    pairs_ref, lab_ref, labs_ref, bias_ref, cross_ref, w_ref, adj_ref, lt_ref, rt_ref,
    out_ref, lg_ref, rg_ref,
    wide, wf, acc, rtp, lhs, og, fa,
):
    row, col, x, y, z, k = place()
    keep = jnp.int32(0)
    for n in range(pairs_ref.shape[1]):
        hit = jnp.logical_and(pairs_ref[0, n] == row * TI // BLK, pairs_ref[1, n] == col * TJ // BLK)
        keep = jnp.where(hit, jnp.int32(1), keep)
    listed = keep.astype(F32)

    wf[...] = w_ref[...].astype(F32)
    wide[...] = jnp.zeros_like(wide)

    @pl.loop(0, C)
    def _(e):
        we = wf[pl.ds(e, C, stride=C), :].astype(BF16)
        for a in range(G):
            wide[pl.ds(pl.multiple_of(e * G * C + a * C, C), C), a * PW:(a + 1) * PW] = we

    for i in range(TI):
        lhs[(i // G) * TJ:(i // G + 1) * TJ, (i % G) * PW:(i % G + 1) * PW] = (
            adj_ref[i].astype(F32) * listed
        ).astype(BF16)

    @pl.loop(0, C // 4)
    def _(n):
        part = lax.dot_general(
            lhs[...], wide[pl.ds(pl.multiple_of(n * 512, 512), 512), :],
            (((1,), (1,)), ((), ())), preferred_element_type=F32,
        ).astype(BF16)
        for q in range(4):
            for g in range(NG):
                og[pl.ds(pl.multiple_of((n * 4 + q) * TJ, TJ), TJ), g * 128:(g + 1) * 128] = (
                    part[g * TJ:(g + 1) * TJ, q * 128:(q + 1) * 128]
                )

    acc[...] = rt_ref[...].astype(F32)

    @pl.loop(0, C)
    def _(e):
        rtp[pl.ds(pl.multiple_of(e * TJ, TJ), TJ), :] = acc[pl.ds(e, TJ, stride=C), :].astype(BF16)

    @pl.loop(0, 4)
    def _(n):
        rows = pl.ds(pl.multiple_of(n * 512, 512), 512)
        acc[rows, :] = jnp.dot(og[rows, :], lt_ref[...], preferred_element_type=F32) * (1.0 / S)

    @pl.loop(0, TJ)
    def _(j):
        rg_ref[pl.ds(pl.multiple_of(j * C, C), C), :] = acc[pl.ds(j, C, stride=TJ), :].astype(BF16)

    r2 = rtp[...].T
    for n in range(4):
        part = jnp.dot(r2, og[:, n * 256:(n + 1) * 256], preferred_element_type=F32) * (1.0 / S)
        lg_ref[n * 256:(n + 1) * 256, :] = part.T.astype(BF16)

    left = lt_ref[...].T

    @pl.loop(0, C // 4)
    def _(n):
        part = (jnp.dot(
            rtp[pl.ds(pl.multiple_of(n * 256, 256), 256), :], left, preferred_element_type=F32,
        ) * (1.0 / S)).astype(BF16)
        for q in range(4):
            for g in range(NG):
                fa[g * TJ:(g + 1) * TJ, pl.ds(pl.multiple_of((n * 4 + q) * 128, 128), 128)] = (
                    part[q * TJ:(q + 1) * TJ, g * 128:(g + 1) * 128]
                )

    labels = down(lab_ref[pl.ds(z, 1), :], PW)
    mine = jnp.where(k == 0, labels[:TJ], labels[TJ:])
    bias = bias_ref[...] * listed
    cross = cross_ref[...] * listed

    @pl.loop(0, NG)
    def _(g):
        part = jnp.dot(
            fa[pl.ds(pl.multiple_of(g * TJ, TJ), TJ), :], wide[...], preferred_element_type=F32,
        )
        for a in range(G):
            i = g * G + a
            apart = (mine != labs_ref[row * TI + i]).astype(F32)
            out_ref[i] = (
                part[:, a * PW:(a + 1) * PW] * listed + bias + cross * apart
            ).astype(BF16)


def reduce_kernel(
    lg_ref, rg_ref, left_ref, right_ref,
    lx, rx, ry, ys,
    l_send, l_recv, x_send, x_recv, y_send, y_recv,
):
    row, col, x, y, z, k = place()
    barrier = pltpu.get_barrier_semaphore()

    def greet(r, c):
        pl.semaphore_signal(barrier, inc=1, device_id=(r, c), device_id_type=MESH)

    for dx in range(1, NX):
        greet(y * NX + lax.rem(x + dx, NX), col)
    for dy in range(1, NY):
        greet(lax.rem(y + dy, NY) * NX + x, col)
    for dc in range(1, NCOL):
        greet(row, lax.rem(col + dc, NCOL))
    pl.semaphore_wait(barrier, NX - 1 + NY - 1 + NCOL - 1)

    def along_x(dy, dx):
        y2, x2 = lax.rem(y + dy, NY), lax.rem(x + dx, NX)
        return remote(rg_ref.at[y2 * NX + x2], rx.at[dx - 1, dy], x_send.at[dx - 1, dy],
                      x_recv.at[dx - 1, dy], y * NX + x2, col)

    def along_y(dy):
        return remote(ys.at[dy - 1], ry.at[dy - 1], y_send.at[dy - 1], y_recv.at[dy - 1],
                      lax.rem(y + dy, NY) * NX + x, col)

    def along_col(dc):
        c2 = lax.rem(col + dc, NCOL)
        return remote(lg_ref.at[c2], lx.at[dc - 1], l_send.at[dc - 1], l_recv.at[dc - 1], row, c2)

    order = (4, 3, 5, 2, 6, 1, 7, 0)
    for dy in order:
        for dx in range(1, NX):
            along_x(dy, dx).start()
    for dc in range(1, NCOL):
        along_col(dc).start()

    for dy in order:
        total = rg_ref[lax.rem(y + dy, NY) * NX + x].astype(F32)
        for dx in range(1, NX):
            along_x(dy, dx).wait_recv()
            total = total + rx[dx - 1, dy].astype(F32)
        if dy:
            ys[dy - 1] = total.astype(BF16)
            along_y(dy).start()
        else:
            right_ref[...] = total

    total = lg_ref[col].astype(F32)
    for dc in range(1, NCOL):
        along_col(dc).wait_recv()
        total = total + lx[dc - 1].astype(F32)
    left_ref[...] = total

    total = right_ref[...]
    for dy in range(1, NY):
        along_y(dy).wait_recv()
        total = total + ry[dy - 1].astype(F32)
    right_ref[...] = total

    for dy in range(NY):
        for dx in range(1, NX):
            along_x(dy, dx).wait_send()
        if dy:
            along_y(dy).wait_send()
    for dc in range(1, NCOL):
        along_col(dc).wait_send()


def vmem():
    return pl.BlockSpec(memory_space=pltpu.VMEM)


def smem():
    return pl.BlockSpec(memory_space=pltpu.SMEM)


def per_device(
    sequence_features, standardize_scale, standardize_shift,
    first_projection_kernel, first_projection_shift,
    second_projection_kernel, second_projection_shift,
    final_projection_kernel, final_projection_shift, cross_molecule_shift,
    residue_molecule_label, selected_tile_couples, result_adjoint,
):
    dma = pltpu.SemaphoreType.DMA
    lt, rt = pl.pallas_call(
        gather_kernel,
        out_shape=(
            jax.ShapeDtypeStruct((TI * C, S), BF16),
            jax.ShapeDtypeStruct((TJ * C, S), BF16),
        ),
        in_specs=[vmem()] * 7,
        out_specs=(vmem(), vmem()),
        scratch_shapes=[
            pltpu.VMEM((2, OWN, S), BF16),
            pltpu.VMEM((NZ, OWN, S), BF16),
            dma((NZ,)), dma((NZ,)), dma((NCOL,)),
            dma((NY,)), dma((NZ,)),
            dma((NY, NX)), dma((2 * NCOL,)),
        ],
        compiler_params=pltpu.CompilerParams(
            collective_id=0, has_side_effects=True, vmem_limit_bytes=16 * 2**20
        ),
        name="gather_factors",
    )(
        sequence_features.transpose(1, 2, 0),
        standardize_scale[None], standardize_shift[None],
        first_projection_kernel.T, first_projection_shift[None],
        second_projection_kernel.T, second_projection_shift[None],
    )

    pair, lg, rg = pl.pallas_call(
        tile_kernel,
        out_shape=(
            jax.ShapeDtypeStruct((TI, TJ, PW), BF16),
            jax.ShapeDtypeStruct((TI * C, S), BF16),
            jax.ShapeDtypeStruct((TJ * C, S), BF16),
        ),
        in_specs=[smem(), vmem(), smem()] + [vmem()] * 6,
        out_specs=(vmem(), vmem(), vmem()),
        scratch_shapes=[
            pltpu.VMEM((C * G * C, G * PW), BF16),
            pltpu.VMEM((C * C, PW), F32),
            pltpu.VMEM((TJ * C, S), F32),
            pltpu.VMEM((TJ * C, S), BF16),
            pltpu.VMEM((NG * TJ, G * PW), BF16),
            pltpu.VMEM((C * TJ, TI * C), BF16),
            pltpu.VMEM((NG * TJ, C * G * C), BF16),
        ],
        compiler_params=pltpu.CompilerParams(vmem_limit_bytes=48 * 2**20),
        name="pair_tile",
    )(
        selected_tile_couples.T, residue_molecule_label.reshape(8, 128), residue_molecule_label,
        final_projection_shift[None], cross_molecule_shift[None],
        final_projection_kernel, result_adjoint, lt, rt,
    )

    left, right = pl.pallas_call(
        reduce_kernel,
        out_shape=(
            jax.ShapeDtypeStruct((OWN, S), F32),
            jax.ShapeDtypeStruct((OWN, S), F32),
        ),
        in_specs=[vmem()] * 2,
        out_specs=(vmem(), vmem()),
        scratch_shapes=[
            pltpu.VMEM((NCOL - 1, OWN, S), BF16),
            pltpu.VMEM((NX - 1, NY, OWN, S), BF16),
            pltpu.VMEM((NY - 1, OWN, S), BF16),
            pltpu.VMEM((NY - 1, OWN, S), BF16),
            dma((NCOL - 1,)), dma((NCOL - 1,)),
            dma((NX - 1, NY)), dma((NX - 1, NY)),
            dma((NY - 1,)), dma((NY - 1,)),
        ],
        compiler_params=pltpu.CompilerParams(
            collective_id=1, has_side_effects=True, vmem_limit_bytes=16 * 2**20
        ),
        name="reduce_gradients",
    )(lg.reshape(NCOL, OWN, S), rg.reshape(NX * NY, OWN, S))

    def back(grad):
        return grad.reshape(2, C, S).transpose(2, 0, 1)

    return pair, back(left), back(right)


def solution(mesh):
    placed = (P(None, ("row", "col"), None),) + (P(),) * 11 + (P("row", "col", None),)
    return jax.shard_map(
        per_device,
        mesh=mesh,
        in_specs=placed,
        out_specs=(
            P("row", "col", None),
            P(None, ("row", "col"), None),
            P(None, ("col", "row"), None),
        ),
        check_vma=False,
    )
```

```python
import jax
import jax.numpy as jnp
from jax import lax
from jax.experimental import pallas as pl
from jax.experimental.pallas import tpu as pltpu
from jax.sharding import PartitionSpec as P

F32 = jnp.float32
BF16 = jnp.bfloat16
MESH = pl.DeviceIdType.MESH

NX, NY, NZ, NK = 4, 8, 8, 2
NCOL = NZ * NK
S = 128
C = 32
PW = 128
TI = 32
TJ = 64
OWN = 2 * C
G = 4
NG = TI // G
BLK = 128
FEATURES = 64
LISTED = 16
TOKENS = 1024


def place():
    row, col = lax.axis_index("row"), lax.axis_index("col")
    return row, col, row % NX, row // NX, col // NK, col % NK


def remote(src, dst, send, recv, row, col):
    return pltpu.make_async_remote_copy(
        src_ref=src, dst_ref=dst, send_sem=send, recv_sem=recv,
        device_id=(row, col), device_id_type=MESH,
    )


def down(vector, width):
    return jnp.broadcast_to(vector, (width, vector.shape[1])).T


NEAR = (0, 1, 7, 2, 6, 3, 5, 4)
FAR = (4, 3, 5, 2, 6, 1, 7)
JC = 16


def kernel(
    x_hbm, gain_hbm, shift_hbm, w1_hbm, b1_hbm, w2_hbm, b2_hbm,
    w_hbm, pairs_hbm, adj_hbm, labs_hbm, lab_hbm, bias_hbm, cross_hbm,
    out_ref, grads_ref,
    x_ref, gain_ref, shift_ref, w1_ref, b1_ref, w2_ref, b2_ref,
    w_ref, pairs_ref, adj_ref, labs_ref, lab_ref, bias_ref, cross_ref,
    own, ystage, zstage, lt, rt, wide, wf, acc, rtp, lhs, og, fa,
    lg, rg, lx, rx, ry, ys,
    in_sem, l_send, l_fwd, l_recv, y_send, y_recv, z_send, z_recv, r_send, r_recv,
    lg_send, lg_recv, gx_send, gx_recv, gy_send, gy_recv,
):
    row, col, x, y, z, k = place()
    home = x // 2
    loads = [
        pltpu.make_async_copy(src, dst, in_sem.at[n])
        for n, (src, dst) in enumerate((
            (x_hbm, x_ref), (gain_hbm, gain_ref), (shift_hbm, shift_ref),
            (w1_hbm, w1_ref), (b1_hbm, b1_ref), (w2_hbm, w2_ref), (b2_hbm, b2_ref),
            (w_hbm, w_ref), (pairs_hbm, pairs_ref), (adj_hbm, adj_ref),
            (labs_hbm, labs_ref), (lab_hbm, lab_ref), (bias_hbm, bias_ref), (cross_hbm, cross_ref),
        ))
    ]
    for load in loads:
        load.start()
    barrier = pltpu.get_barrier_semaphore()

    def greet(r, c):
        pl.semaphore_signal(barrier, inc=1, device_id=(r, c), device_id_type=MESH)

    for dc in range(1, NCOL):
        greet(row, lax.rem(col + dc, NCOL))
    for dy in range(1, NY):
        greet(lax.rem(y + dy, NY) * NX + x, col)
    for dx in range(1, NX):
        for kk in range(NK):
            greet(y * NX + lax.rem(x + dx, NX), z * NK + kk)

    for load in loads[:7]:
        load.wait()
    gain = down(gain_ref[...], S)
    shift = down(shift_ref[...], S)
    b1 = down(b1_ref[...], S)
    b2 = down(b2_ref[...], S)
    for t in range(2):
        v = x_ref[t].astype(F32)
        mean = jnp.mean(v, axis=0, keepdims=True)
        var = jnp.mean((v - mean) ** 2, axis=0, keepdims=True)
        n = ((v - mean) * lax.rsqrt(var + 1e-05) * gain + shift).astype(BF16)
        own[0, t * C:(t + 1) * C, :] = (
            jnp.dot(w1_ref[...], n, preferred_element_type=F32) + b1
        ).astype(BF16)
        own[1, t * C:(t + 1) * C, :] = (
            jnp.dot(w2_ref[...], n, preferred_element_type=F32) + b2
        ).astype(BF16)

    wide[...] = jnp.zeros_like(wide)
    loads[7].wait()
    wf[...] = w_ref[...].astype(F32)

    @pl.loop(0, C)
    def _(e):
        we = wf[pl.ds(e, C, stride=C), :].astype(BF16)
        for a in range(G):
            wide[pl.ds(pl.multiple_of(e * G * C + a * C, C), C), a * PW:(a + 1) * PW] = we

    for load in loads[8:]:
        load.wait()
    hits = jnp.int32(0)
    for n in range(pairs_ref.shape[1]):
        hits = hits + (pairs_ref[0, n] == y).astype(jnp.int32) * (
            pairs_ref[1, n] == z
        ).astype(jnp.int32)
    listed = hits.astype(F32)
    for i in range(TI):
        lhs[(i // G) * TJ:(i // G + 1) * TJ, (i % G) * PW:(i % G + 1) * PW] = (
            adj_ref[i].astype(F32) * listed
        ).astype(BF16)

    pl.semaphore_wait(barrier, NCOL - 1 + NY - 1 + NK * (NX - 1))

    def block(ref, index):
        return ref.at[pl.ds(pl.multiple_of(index * OWN, OWN), OWN), :]

    def arrived(ref, sem):
        pltpu.make_async_copy(ref, ref, sem).wait()

    def leg_y(d):
        return remote(own.at[1], ystage.at[y], y_send.at[d], y_recv.at[y],
                      lax.rem(y + d, NY) * NX + x, col)

    def leg_z(d):
        y2 = lax.rem(y + d, NY)
        return remote(ystage.at[y2], zstage.at[z], z_send.at[d], z_recv.at[z],
                      row, y2 * NK + k)

    def leg_x(d, dx):
        slot = lax.rem(z + d, NZ)
        b = (x % 2) * NCOL + slot * NK + k
        return remote(zstage.at[slot], block(rt, b), r_send.at[d, dx], r_recv.at[b],
                      y * NX + lax.rem(x + dx, NX), z * NK + home)

    def left(d):
        c2 = lax.rem(z + d, NZ) * NK + k if d else z * NK + 1 - k
        return remote(own.at[0], block(lt, col), l_send.at[d], l_recv.at[col], row, c2)

    def pass_on(d):
        c2 = lax.rem(z + d, NZ) * NK + k
        return remote(block(lt, c2), block(lt, c2), l_fwd.at[d], l_recv.at[c2],
                      row, z * NK + 1 - k)

    for d in FAR:
        leg_y(d).start()
        left(d).start()
    left(0).start()
    ystage[y] = own[1]
    lt[pl.ds(pl.multiple_of(col * OWN, OWN), OWN), :] = own[0]

    @pl.loop(0, C // 4)
    def _(n):
        part = lax.dot_general(
            lhs[...], wide[pl.ds(pl.multiple_of(n * 512, 512), 512), :],
            (((1,), (1,)), ((), ())), preferred_element_type=F32,
        ).astype(BF16)
        for q in range(4):
            for g in range(NG):
                og[n * 4 + q, :, g * 128:(g + 1) * 128] = (
                    part[g * TJ:(g + 1) * TJ, q * 128:(q + 1) * 128]
                )

    for d in NEAR:
        y2 = lax.rem(y + d, NY)
        if d:
            arrived(ystage.at[y2], y_recv.at[y2])

        @pl.when(y2 != z)
        def _():
            leg_z(d).start()

        @pl.when(y2 == z)
        def _():
            zstage[z] = ystage[z]

    for d in NEAR:
        if d:
            c2 = lax.rem(z + d, NZ) * NK + k
            arrived(block(lt, c2), l_recv.at[c2])
            pass_on(d).start()
    for zz in range(NZ):
        c2 = zz * NK + 1 - k
        arrived(block(lt, c2), l_recv.at[c2])

    def grad_x(y2, dx):
        x2 = lax.rem(x + dx, NX)
        return remote(rg.at[y2 * NX + x2], rx.at[dx - 1, y2], gx_send.at[dx - 1, y2],
                      gx_recv.at[dx - 1, y2], y * NX + x2, col)

    for n in range(TJ // JC):
        acc[...] = jnp.dot(
            og[:, n * JC:(n + 1) * JC, :].reshape(C * JC, TI * C), lt[...],
            preferred_element_type=F32,
        ) * (1.0 / S)
        for j in range(JC):
            at = n * JC + j
            rg[at // 2, (at % 2) * C:(at % 2 + 1) * C, :] = (
                acc[pl.ds(j, C, stride=JC), :].astype(BF16)
            )

    for d in NEAR:
        slot = lax.rem(z + d, NZ)
        if d:
            arrived(zstage.at[slot], z_recv.at[slot])
        for dx in range(1, NX):
            leg_x(d, dx).start()

        @pl.when(home != k)
        def _():
            leg_x(d, 0).start()

        @pl.when(home == k)
        def _():
            b = (x % 2) * NCOL + slot * NK + k
            rt[pl.ds(pl.multiple_of(b * OWN, OWN), OWN), :] = zstage[slot]

    for y2 in range(NY):
        for dx in range(1, NX):
            grad_x(y2, dx).start()

    left_t = lt[...].T
    for xx in range(2):
        for kk in range(NK):
            @pl.when(jnp.logical_or(2 * k + xx != x, kk != k))
            def _(xx=xx, kk=kk):
                for zz in range(NZ):
                    b = xx * NCOL + zz * NK + kk
                    arrived(block(rt, b), r_recv.at[b])

    wide_acc = wf
    for h in range(2):
        wide_acc[...] = rt[h * TI * C:(h + 1) * TI * C, :].astype(F32)
        for e in range(C):
            rtp[e * TJ + h * TI:e * TJ + (h + 1) * TI, :] = (
                wide_acc[pl.ds(e, TI, stride=C), :].astype(BF16)
            )

    right_t = rtp[...].T

    def grad_col(dc):
        c2 = lax.rem(col + dc, NCOL)
        return remote(lg.at[c2], lx.at[dc - 1], lg_send.at[dc - 1], lg_recv.at[dc - 1], row, c2)

    for n in range(4):
        part = jnp.dot(
            right_t, og[:, :, n * 256:(n + 1) * 256].reshape(C * TJ, 256),
            preferred_element_type=F32,
        ) * (1.0 / S)
        lg[n * 4:(n + 1) * 4] = part.T.astype(BF16).reshape(4, OWN, S)
    for dc in range(1, NCOL):
        grad_col(dc).start()

    def grad_y(y2):
        return remote(ys.at[y2], ry.at[y], gy_send.at[y2], gy_recv.at[y], y2 * NX + x, col)

    for y2 in range(NY):
        total = rg[y2 * NX + x].astype(F32)
        for dx in range(1, NX):
            grad_x(y2, dx).wait_recv()
            total = total + rx[dx - 1, y2].astype(F32)

        @pl.when(y2 != y)
        def _():
            ys[y2] = total.astype(BF16)
            grad_y(y2).start()

        @pl.when(y2 == y)
        def _():
            grads_ref[1] = total

    @pl.loop(0, C // 4)
    def _(n):
        part = (jnp.dot(
            rtp[pl.ds(pl.multiple_of(n * 256, 256), 256), :], left_t, preferred_element_type=F32,
        ) * (1.0 / S)).astype(BF16)
        for q in range(4):
            for g in range(NG):
                fa[g * TJ:(g + 1) * TJ, pl.ds(pl.multiple_of((n * 4 + q) * 128, 128), 128)] = (
                    part[q * TJ:(q + 1) * TJ, g * 128:(g + 1) * 128]
                )

    labels = down(lab_ref[pl.ds(z, 1), :], PW)
    mine = jnp.where(k == 0, labels[:TJ], labels[TJ:])
    bias = bias_ref[...] * listed
    cross = cross_ref[...] * listed
    for h in range(2):
        part = jnp.dot(fa[...], wide[:, h * 256:(h + 1) * 256], preferred_element_type=F32)
        for g in range(NG):
            for a in range(2):
                i = g * G + h * 2 + a
                apart = (mine != labs_ref[row * TI + i]).astype(F32)
                out_ref[i] = (
                    part[g * TJ:(g + 1) * TJ, a * PW:(a + 1) * PW] * listed + bias + cross * apart
                ).astype(BF16)

    total = lg[col].astype(F32)
    for dc in range(1, NCOL):
        grad_col(dc).wait_recv()
        total = total + lx[dc - 1].astype(F32)
    grads_ref[0] = total

    total = grads_ref[1]
    for d in range(1, NY):
        y2 = lax.rem(y + d, NY)
        arrived(ry.at[y2], gy_recv.at[y2])
        total = total + ry[y2].astype(F32)
    grads_ref[1] = total

    for d in range(NY):
        left(d).wait_send()
        if d:
            leg_y(d).wait_send()
            pass_on(d).wait_send()
        for dx in range(1, NX):
            leg_x(d, dx).wait_send()
            grad_x(d, dx).wait_send()

        @pl.when(lax.rem(y + d, NY) != z)
        def _():
            leg_z(d).wait_send()

        @pl.when(home != k)
        def _():
            leg_x(d, 0).wait_send()

        @pl.when(d != y)
        def _():
            grad_y(d).wait_send()
    for dc in range(1, NCOL):
        grad_col(dc).wait_send()


def vmem():
    return pl.BlockSpec(memory_space=pltpu.VMEM)


def hbm():
    return pl.BlockSpec(memory_space=pltpu.HBM)


def per_device(
    sequence_features, standardize_scale, standardize_shift,
    first_projection_kernel, first_projection_shift,
    second_projection_kernel, second_projection_shift,
    final_projection_kernel, final_projection_shift, cross_molecule_shift,
    residue_molecule_label, selected_tile_couples, result_adjoint,
):
    dma = pltpu.SemaphoreType.DMA
    block = (OWN, S)
    pair, grads = pl.pallas_call(
        kernel,
        out_shape=(
            jax.ShapeDtypeStruct((TI, TJ, PW), BF16),
            jax.ShapeDtypeStruct((2, OWN, S), F32),
        ),
        in_specs=[hbm()] * 14,
        out_specs=(vmem(), vmem()),
        scratch_shapes=[
            pltpu.VMEM((2, FEATURES, S), BF16),
            pltpu.VMEM((1, FEATURES), F32),
            pltpu.VMEM((1, FEATURES), F32),
            pltpu.VMEM((C, FEATURES), BF16),
            pltpu.VMEM((1, C), F32),
            pltpu.VMEM((C, FEATURES), BF16),
            pltpu.VMEM((1, C), F32),
            pltpu.VMEM((C * C, PW), BF16),
            pltpu.SMEM((2, LISTED), jnp.int32),
            pltpu.VMEM((TI, TJ, PW), BF16),
            pltpu.SMEM((TOKENS,), jnp.int32),
            pltpu.VMEM((NZ, BLK), jnp.int32),
            pltpu.VMEM((1, PW), F32),
            pltpu.VMEM((1, PW), F32),
            pltpu.VMEM((2,) + block, BF16),
            pltpu.VMEM((NY,) + block, BF16),
            pltpu.VMEM((NZ,) + block, BF16),
            pltpu.VMEM((TI * C, S), BF16),
            pltpu.VMEM((TJ * C, S), BF16),
            pltpu.VMEM((C * G * C, G * PW), BF16),
            pltpu.VMEM((C * C, PW), F32),
            pltpu.VMEM((C * JC, S), F32),
            pltpu.VMEM((TJ * C, S), BF16),
            pltpu.VMEM((NG * TJ, G * PW), BF16),
            pltpu.VMEM((C, TJ, TI * C), BF16),
            pltpu.VMEM((NG * TJ, C * G * C), BF16),
            pltpu.VMEM((NCOL,) + block, BF16),
            pltpu.VMEM((NX * NY,) + block, BF16),
            pltpu.VMEM((NCOL - 1,) + block, BF16),
            pltpu.VMEM((NX - 1, NY) + block, BF16),
            pltpu.VMEM((NY,) + block, BF16),
            pltpu.VMEM((NY,) + block, BF16),
            dma((14,)),
            dma((NZ,)), dma((NZ,)), dma((NCOL,)),
            dma((NY,)), dma((NY,)), dma((NY,)), dma((NZ,)),
            dma((NZ, NX)), dma((2 * NCOL,)),
            dma((NCOL - 1,)), dma((NCOL - 1,)),
            dma((NX - 1, NY)), dma((NX - 1, NY)),
            dma((NY,)), dma((NY,)),
        ],
        compiler_params=pltpu.CompilerParams(
            collective_id=0, has_side_effects=True, vmem_limit_bytes=60 * 2**20
        ),
        name="pair_block",
    )(
        sequence_features.transpose(1, 2, 0),
        standardize_scale[None], standardize_shift[None],
        first_projection_kernel.T, first_projection_shift[None],
        second_projection_kernel.T, second_projection_shift[None],
        final_projection_kernel, selected_tile_couples.T, result_adjoint,
        residue_molecule_label, residue_molecule_label.reshape(NZ, BLK),
        final_projection_shift[None], cross_molecule_shift[None],
    )

    def back(grad):
        return grad.reshape(2, C, S).transpose(2, 0, 1)

    return pair, back(grads[0]), back(grads[1])


def solution(mesh):
    placed = (P(None, ("row", "col"), None),) + (P(),) * 11 + (P("row", "col", None),)
    return jax.shard_map(
        per_device,
        mesh=mesh,
        in_specs=placed,
        out_specs=(
            P("row", "col", None),
            P(None, ("row", "col"), None),
            P(None, ("col", "row"), None),
        ),
        check_vma=False,
    )
```

```python
import jax
import jax.numpy as jnp
from jax import lax
from jax.experimental import pallas as pl
from jax.experimental.pallas import tpu as pltpu
from jax.sharding import PartitionSpec as P

F32 = jnp.float32
BF16 = jnp.bfloat16
MESH = pl.DeviceIdType.MESH

NX, NY, NZ, NK = 4, 8, 8, 2
NCOL = NZ * NK
S = 128
C = 32
PW = 128
TI = 32
TJ = 64
OWN = 2 * C
G = 4
NG = TI // G
BLK = 128
FEATURES = 64
LISTED = 16
TOKENS = 1024


def place():
    row, col = lax.axis_index("row"), lax.axis_index("col")
    return row, col, row % NX, row // NX, col // NK, col % NK


def remote(src, dst, send, recv, row, col):
    return pltpu.make_async_remote_copy(
        src_ref=src, dst_ref=dst, send_sem=send, recv_sem=recv,
        device_id=(row, col), device_id_type=MESH,
    )


def down(vector, width):
    return jnp.broadcast_to(vector, (width, vector.shape[1])).T


NEAR = (0, 1, 7, 2, 6, 3, 5, 4)
FAR = (4, 3, 5, 2, 6, 1, 7)
JC = 16


def kernel(
    x_hbm, gain_hbm, shift_hbm, w1_hbm, b1_hbm, w2_hbm, b2_hbm,
    w_hbm, pairs_hbm, adj_hbm, labs_hbm, lab_hbm, bias_hbm, cross_hbm,
    out_hbm, grads_hbm,
    x_ref, gain_ref, shift_ref, w1_ref, b1_ref, w2_ref, b2_ref,
    w_ref, pairs_ref, adj_ref, labs_ref, lab_ref, bias_ref, cross_ref,
    own, ystage, zstage, lt, rt, wide, wf, acc, rtp, lhs, og, fa,
    lg, rg, lx, rx, ry, ys, pair, sums,
    in_sem, out_sem, l_send, l_fwd, l_recv, y_send, y_recv, z_send, z_recv, r_send, r_recv,
    lg_send, lg_recv, gx_send, gx_recv, gy_send, gy_recv,
):
    row, col, x, y, z, k = place()
    home = x // 2
    loads = [
        pltpu.make_async_copy(src, dst, in_sem.at[n])
        for n, (src, dst) in enumerate((
            (x_hbm, x_ref), (gain_hbm, gain_ref), (shift_hbm, shift_ref),
            (w1_hbm, w1_ref), (b1_hbm, b1_ref), (w2_hbm, w2_ref), (b2_hbm, b2_ref),
            (w_hbm, w_ref), (pairs_hbm, pairs_ref), (adj_hbm, adj_ref),
            (labs_hbm, labs_ref), (lab_hbm, lab_ref), (bias_hbm, bias_ref), (cross_hbm, cross_ref),
        ))
    ]
    for load in loads:
        load.start()
    barrier = pltpu.get_barrier_semaphore()

    def greet(r, c):
        pl.semaphore_signal(barrier, inc=1, device_id=(r, c), device_id_type=MESH)

    for dc in range(1, NCOL):
        greet(row, lax.rem(col + dc, NCOL))
    for dy in range(1, NY):
        greet(lax.rem(y + dy, NY) * NX + x, col)
    for dx in range(1, NX):
        for kk in range(NK):
            greet(y * NX + lax.rem(x + dx, NX), z * NK + kk)

    for load in loads[:7]:
        load.wait()
    gain = down(gain_ref[...], S)
    shift = down(shift_ref[...], S)
    b1 = down(b1_ref[...], S)
    b2 = down(b2_ref[...], S)
    for t in range(2):
        v = x_ref[t].astype(F32)
        mean = jnp.mean(v, axis=0, keepdims=True)
        var = jnp.mean((v - mean) ** 2, axis=0, keepdims=True)
        n = ((v - mean) * lax.rsqrt(var + 1e-05) * gain + shift).astype(BF16)
        own[0, t * C:(t + 1) * C, :] = (
            jnp.dot(w1_ref[...], n, preferred_element_type=F32) + b1
        ).astype(BF16)
        own[1, t * C:(t + 1) * C, :] = (
            jnp.dot(w2_ref[...], n, preferred_element_type=F32) + b2
        ).astype(BF16)

    pl.semaphore_wait(barrier, NCOL - 1 + NY - 1 + NK * (NX - 1))

    def block(ref, index):
        return ref.at[pl.ds(pl.multiple_of(index * OWN, OWN), OWN), :]

    def arrived(ref, sem):
        pltpu.make_async_copy(ref, ref, sem).wait()

    def leg_y(d):
        return remote(own.at[1], ystage.at[y], y_send.at[d], y_recv.at[y],
                      lax.rem(y + d, NY) * NX + x, col)

    def leg_z(d):
        y2 = lax.rem(y + d, NY)
        return remote(ystage.at[y2], zstage.at[z], z_send.at[d], z_recv.at[z],
                      row, y2 * NK + k)

    def leg_x(d, dx):
        slot = lax.rem(z + d, NZ)
        b = (x % 2) * NCOL + slot * NK + k
        return remote(zstage.at[slot], block(rt, b), r_send.at[d, dx], r_recv.at[b],
                      y * NX + lax.rem(x + dx, NX), z * NK + home)

    def left(d):
        c2 = lax.rem(z + d, NZ) * NK + k if d else z * NK + 1 - k
        return remote(own.at[0], block(lt, col), l_send.at[d], l_recv.at[col], row, c2)

    def pass_on(d):
        c2 = lax.rem(z + d, NZ) * NK + k
        return remote(block(lt, c2), block(lt, c2), l_fwd.at[d], l_recv.at[c2],
                      row, z * NK + 1 - k)

    def turn_z(d):
        y2 = lax.rem(y + d, NY)
        if d:
            arrived(ystage.at[y2], y_recv.at[y2])

        @pl.when(y2 != z)
        def _():
            leg_z(d).start()

        @pl.when(y2 == z)
        def _():
            zstage[z] = ystage[z]

    def turn_x(d):
        slot = lax.rem(z + d, NZ)
        if d:
            arrived(zstage.at[slot], z_recv.at[slot])
        for dx in range(1, NX):
            leg_x(d, dx).start()

        @pl.when(home != k)
        def _():
            leg_x(d, 0).start()

        @pl.when(home == k)
        def _():
            b = (x % 2) * NCOL + slot * NK + k
            rt[pl.ds(pl.multiple_of(b * OWN, OWN), OWN), :] = zstage[slot]

    def share(d):
        c2 = lax.rem(z + d, NZ) * NK + k
        arrived(block(lt, c2), l_recv.at[c2])
        pass_on(d).start()

    for d in FAR:
        leg_y(d).start()
        left(d).start()
    left(0).start()
    ystage[y] = own[1]
    lt[pl.ds(pl.multiple_of(col * OWN, OWN), OWN), :] = own[0]
    turn_z(0)

    wide[...] = jnp.zeros_like(wide)
    loads[7].wait()
    wf[...] = w_ref[...].astype(F32)

    @pl.loop(0, C)
    def _(e):
        we = wf[pl.ds(e, C, stride=C), :].astype(BF16)
        for a in range(G):
            wide[pl.ds(pl.multiple_of(e * G * C + a * C, C), C), a * PW:(a + 1) * PW] = we

    for load in loads[8:]:
        load.wait()
    hits = jnp.int32(0)
    for n in range(pairs_ref.shape[1]):
        hits = hits + (pairs_ref[0, n] == y).astype(jnp.int32) * (
            pairs_ref[1, n] == z
        ).astype(jnp.int32)
    listed = hits.astype(F32)
    for i in range(TI):
        lhs[(i // G) * TJ:(i // G + 1) * TJ, (i % G) * PW:(i % G + 1) * PW] = (
            adj_ref[i].astype(F32) * listed
        ).astype(BF16)

    def outer_grad(first, last):
        @pl.loop(first, last)
        def _(n):
            part = lax.dot_general(
                lhs[...], wide[pl.ds(pl.multiple_of(n * 512, 512), 512), :],
                (((1,), (1,)), ((), ())), preferred_element_type=F32,
            ).astype(BF16)
            for q in range(4):
                for g in range(NG):
                    og[n * 4 + q, :, g * 128:(g + 1) * 128] = (
                        part[g * TJ:(g + 1) * TJ, q * 128:(q + 1) * 128]
                    )

    outer_grad(0, 8)
    for d in NEAR[1:]:
        turn_z(d)
    for d in NEAR[1:]:
        share(d)
    for zz in range(NZ):
        c2 = zz * NK + 1 - k
        arrived(block(lt, c2), l_recv.at[c2])

    def grad_x(y2, dx):
        x2 = lax.rem(x + dx, NX)
        return remote(rg.at[y2 * NX + x2], rx.at[dx - 1, y2], gx_send.at[dx - 1, y2],
                      gx_recv.at[dx - 1, y2], y * NX + x2, col)

    for n in range(TJ // JC):
        acc[...] = jnp.dot(
            og[:, n * JC:(n + 1) * JC, :].reshape(C * JC, TI * C), lt[...],
            preferred_element_type=F32,
        ) * (1.0 / S)
        for j in range(JC):
            at = n * JC + j
            rg[at // 2, (at % 2) * C:(at % 2 + 1) * C, :] = (
                acc[pl.ds(j, C, stride=JC), :].astype(BF16)
            )

    for d in NEAR:
        turn_x(d)
    for y2 in range(NY):
        for dx in range(1, NX):
            grad_x(y2, dx).start()

    left_t = lt[...].T
    for xx in range(2):
        for kk in range(NK):
            @pl.when(jnp.logical_or(2 * k + xx != x, kk != k))
            def _(xx=xx, kk=kk):
                for zz in range(NZ):
                    b = xx * NCOL + zz * NK + kk
                    arrived(block(rt, b), r_recv.at[b])

    for h in range(2):
        wf[...] = rt[h * TI * C:(h + 1) * TI * C, :].astype(F32)
        for e in range(C):
            rtp[e * TJ + h * TI:e * TJ + (h + 1) * TI, :] = (
                wf[pl.ds(e, TI, stride=C), :].astype(BF16)
            )

    right_t = rtp[...].T

    def grad_col(c2):
        return remote(lg.at[c2], lx.at[col], lg_send.at[c2], lg_recv.at[col], row, c2)

    for n in range(4):
        part = jnp.dot(
            right_t, og[:, :, n * 256:(n + 1) * 256].reshape(C * TJ, 256),
            preferred_element_type=F32,
        ) * (1.0 / S)
        lg[n * 4:(n + 1) * 4] = part.T.astype(BF16).reshape(4, OWN, S)
        for c2 in range(4 * n, 4 * n + 4):
            @pl.when(c2 != col)
            def _(c2=c2):
                grad_col(c2).start()

    def grad_y(y2):
        return remote(ys.at[y2], ry.at[y], gy_send.at[y2], gy_recv.at[y], y2 * NX + x, col)

    for y2 in range(NY):
        total = rg[y2 * NX + x].astype(F32)
        for dx in range(1, NX):
            grad_x(y2, dx).wait_recv()
            total = total + rx[dx - 1, y2].astype(F32)

        @pl.when(y2 != y)
        def _():
            ys[y2] = total.astype(BF16)
            grad_y(y2).start()

        @pl.when(y2 == y)
        def _():
            sums[1] = total

    @pl.loop(0, C // 4)
    def _(n):
        part = (jnp.dot(
            rtp[pl.ds(pl.multiple_of(n * 256, 256), 256), :], left_t, preferred_element_type=F32,
        ) * (1.0 / S)).astype(BF16)
        for q in range(4):
            for g in range(NG):
                fa[g * TJ:(g + 1) * TJ, pl.ds(pl.multiple_of((n * 4 + q) * 128, 128), 128)] = (
                    part[q * TJ:(q + 1) * TJ, g * 128:(g + 1) * 128]
                )

    labels = down(lab_ref[pl.ds(z, 1), :], PW)
    mine = jnp.where(k == 0, labels[:TJ], labels[TJ:])
    bias = bias_ref[...] * listed
    cross = cross_ref[...] * listed
    for h in range(2):
        part = jnp.dot(fa[...], wide[:, h * 256:(h + 1) * 256], preferred_element_type=F32)
        for g in range(NG):
            for a in range(2):
                i = g * G + h * 2 + a
                apart = (mine != labs_ref[row * TI + i]).astype(F32)
                pair[i] = (
                    part[g * TJ:(g + 1) * TJ, a * PW:(a + 1) * PW] * listed + bias + cross * apart
                ).astype(BF16)

    pair_copy = pltpu.make_async_copy(pair, out_hbm, out_sem.at[0])
    pair_copy.start()

    total = lg[col].astype(F32)
    for d in range(1, NCOL):
        c2 = lax.rem(col + d, NCOL)
        arrived(lx.at[c2], lg_recv.at[c2])
        total = total + lx[c2].astype(F32)
    sums[0] = total

    total = sums[1]
    for d in range(1, NY):
        y2 = lax.rem(y + d, NY)
        arrived(ry.at[y2], gy_recv.at[y2])
        total = total + ry[y2].astype(F32)
    sums[1] = total

    sums_copy = pltpu.make_async_copy(sums, grads_hbm, out_sem.at[1])
    sums_copy.start()

    for d in range(NY):
        left(d).wait_send()
        if d:
            leg_y(d).wait_send()
            pass_on(d).wait_send()
        for dx in range(1, NX):
            leg_x(d, dx).wait_send()
            grad_x(d, dx).wait_send()

        @pl.when(lax.rem(y + d, NY) != z)
        def _():
            leg_z(d).wait_send()

        @pl.when(home != k)
        def _():
            leg_x(d, 0).wait_send()

        @pl.when(d != y)
        def _():
            grad_y(d).wait_send()
    for c2 in range(NCOL):
        @pl.when(c2 != col)
        def _(c2=c2):
            grad_col(c2).wait_send()
    pair_copy.wait()
    sums_copy.wait()


def hand_over(pair_in, grads_in, pair_out, left_out, right_out, pair, grads, sems):
    rows = TI // 4
    moves = [(grads_in.at[n], grads.at[n], out) for n, out in enumerate((left_out, right_out))] + [
        (pair_in.at[part], pair.at[part], pair_out.at[part])
        for part in (pl.ds(n * rows, rows) for n in range(4))
    ]
    ins = [pltpu.make_async_copy(a, b, sems.at[0, n]) for n, (a, b, _) in enumerate(moves)]
    outs = [pltpu.make_async_copy(b, c, sems.at[1, n]) for n, (_, b, c) in enumerate(moves)]
    for copy in ins:
        copy.start()
    for first, then in zip(ins, outs):
        first.wait()
        then.start()
    for copy in outs:
        copy.wait()


def hbm():
    return pl.BlockSpec(memory_space=pltpu.HBM)


def per_device(
    sequence_features, standardize_scale, standardize_shift,
    first_projection_kernel, first_projection_shift,
    second_projection_kernel, second_projection_shift,
    final_projection_kernel, final_projection_shift, cross_molecule_shift,
    residue_molecule_label, selected_tile_couples, result_adjoint,
):
    dma = pltpu.SemaphoreType.DMA
    block = (OWN, S)
    pair, grads = pl.pallas_call(
        kernel,
        out_shape=(
            jax.ShapeDtypeStruct((TI, TJ, PW), BF16),
            jax.ShapeDtypeStruct((2, OWN, S), F32),
        ),
        in_specs=[hbm()] * 14,
        out_specs=(hbm(), hbm()),
        scratch_shapes=[
            pltpu.VMEM((2, FEATURES, S), BF16),
            pltpu.VMEM((1, FEATURES), F32),
            pltpu.VMEM((1, FEATURES), F32),
            pltpu.VMEM((C, FEATURES), BF16),
            pltpu.VMEM((1, C), F32),
            pltpu.VMEM((C, FEATURES), BF16),
            pltpu.VMEM((1, C), F32),
            pltpu.VMEM((C * C, PW), BF16),
            pltpu.SMEM((2, LISTED), jnp.int32),
            pltpu.VMEM((TI, TJ, PW), BF16),
            pltpu.SMEM((TOKENS,), jnp.int32),
            pltpu.VMEM((NZ, BLK), jnp.int32),
            pltpu.VMEM((1, PW), F32),
            pltpu.VMEM((1, PW), F32),
            pltpu.VMEM((2,) + block, BF16),
            pltpu.VMEM((NY,) + block, BF16),
            pltpu.VMEM((NZ,) + block, BF16),
            pltpu.VMEM((TI * C, S), BF16),
            pltpu.VMEM((TJ * C, S), BF16),
            pltpu.VMEM((C * G * C, G * PW), BF16),
            pltpu.VMEM((C * C, PW), F32),
            pltpu.VMEM((C * JC, S), F32),
            pltpu.VMEM((TJ * C, S), BF16),
            pltpu.VMEM((NG * TJ, G * PW), BF16),
            pltpu.VMEM((C, TJ, TI * C), BF16),
            pltpu.VMEM((NG * TJ, C * G * C), BF16),
            pltpu.VMEM((NCOL,) + block, BF16),
            pltpu.VMEM((NX * NY,) + block, BF16),
            pltpu.VMEM((NCOL,) + block, BF16),
            pltpu.VMEM((NX - 1, NY) + block, BF16),
            pltpu.VMEM((NY,) + block, BF16),
            pltpu.VMEM((NY,) + block, BF16),
            pltpu.VMEM((TI, TJ, PW), BF16),
            pltpu.VMEM((2,) + block, F32),
            dma((14,)), dma((2,)),
            dma((NZ,)), dma((NZ,)), dma((NCOL,)),
            dma((NY,)), dma((NY,)), dma((NY,)), dma((NZ,)),
            dma((NZ, NX)), dma((2 * NCOL,)),
            dma((NCOL,)), dma((NCOL,)),
            dma((NX - 1, NY)), dma((NX - 1, NY)),
            dma((NY,)), dma((NY,)),
        ],
        compiler_params=pltpu.CompilerParams(
            collective_id=0, has_side_effects=True, vmem_limit_bytes=60 * 2**20
        ),
        name="pair_block",
    )(
        sequence_features.transpose(1, 2, 0),
        standardize_scale[None], standardize_shift[None],
        first_projection_kernel.T, first_projection_shift[None],
        second_projection_kernel.T, second_projection_shift[None],
        final_projection_kernel, selected_tile_couples.T, result_adjoint,
        residue_molecule_label, residue_molecule_label.reshape(NZ, BLK),
        final_projection_shift[None], cross_molecule_shift[None],
    )

    pair, left, right = pl.pallas_call(
        hand_over,
        out_shape=(
            jax.ShapeDtypeStruct((TI, TJ, PW), BF16),
            jax.ShapeDtypeStruct(block, F32),
            jax.ShapeDtypeStruct(block, F32),
        ),
        in_specs=[hbm()] * 2,
        out_specs=(hbm(),) * 3,
        scratch_shapes=[
            pltpu.VMEM((TI, TJ, PW), BF16),
            pltpu.VMEM((2,) + block, F32),
            dma((2, 6)),
        ],
        compiler_params=pltpu.CompilerParams(vmem_limit_bytes=60 * 2**20),
        name="hand_over",
    )(pair, grads)

    def back(grad):
        return grad.reshape(2, C, S).transpose(2, 0, 1)

    return pair, back(left), back(right)


def solution(mesh):
    placed = (P(None, ("row", "col"), None),) + (P(),) * 11 + (P("row", "col", None),)
    return jax.shard_map(
        per_device,
        mesh=mesh,
        in_specs=placed,
        out_specs=(
            P("row", "col", None),
            P(None, ("row", "col"), None),
            P(None, ("col", "row"), None),
        ),
        check_vma=False,
    )
```

```python
import jax
import jax.numpy as jnp
from jax import lax
from jax.experimental import pallas as pl
from jax.experimental.pallas import tpu as pltpu
from jax.sharding import PartitionSpec as P

F32 = jnp.float32
BF16 = jnp.bfloat16
MESH = pl.DeviceIdType.MESH

NX, NY, NZ, NK = 4, 8, 8, 2
NCOL = NZ * NK
S = 128
C = 32
PW = 128
TI = 32
TJ = 64
OWN = 2 * C
G = 4
NG = TI // G
BLK = 128
FEATURES = 64
LISTED = 16
TOKENS = 1024


def place():
    row, col = lax.axis_index("row"), lax.axis_index("col")
    return row, col, row % NX, row // NX, col // NK, col % NK


def remote(src, dst, send, recv, row, col):
    return pltpu.make_async_remote_copy(
        src_ref=src, dst_ref=dst, send_sem=send, recv_sem=recv,
        device_id=(row, col), device_id_type=MESH,
    )


def down(vector, width):
    return jnp.broadcast_to(vector, (width, vector.shape[1])).T


NEAR = (0, 1, 7, 2, 6, 3, 5, 4)
FAR = (4, 3, 5, 2, 6, 1, 7)
JC = 16


def kernel(
    x_hbm, gain_hbm, shift_hbm, w1_hbm, b1_hbm, w2_hbm, b2_hbm,
    w_hbm, pairs_hbm, adj_hbm, labs_hbm, lab_hbm, bias_hbm, cross_hbm,
    out_hbm, grads_hbm,
    x_ref, gain_ref, shift_ref, w1_ref, b1_ref, w2_ref, b2_ref,
    w_ref, pairs_ref, adj_ref, labs_ref, lab_ref, bias_ref, cross_ref,
    own, ystage, zstage, lt, rt, wide, wf, acc, rtp, lhs, og, fa,
    lg, rg, lx, rx, ry, ys, pair, sums,
    in_sem, out_sem, l_send, l_fwd, l_recv, y_send, y_recv, z_send, z_recv, r_send, r_recv,
    lg_send, lg_recv, gx_send, gx_recv, gy_send, gy_recv,
):
    row, col, x, y, z, k = place()
    home = x // 2
    barrier = pltpu.get_barrier_semaphore()

    def greet(r, c):
        pl.semaphore_signal(barrier, inc=1, device_id=(r, c), device_id_type=MESH)

    for d in FAR:
        greet(lax.rem(y + d, NY) * NX + x, col)
        for kk in range(NK):
            greet(row, lax.rem(z + d, NZ) * NK + kk)
    greet(row, z * NK + 1 - k)
    for dx in range(1, NX):
        for kk in range(NK):
            greet(y * NX + lax.rem(x + dx, NX), z * NK + kk)

    loads = [
        pltpu.make_async_copy(src, dst, in_sem.at[n])
        for n, (src, dst) in enumerate((
            (x_hbm, x_ref), (gain_hbm, gain_ref), (shift_hbm, shift_ref),
            (w1_hbm, w1_ref), (b1_hbm, b1_ref), (w2_hbm, w2_ref), (b2_hbm, b2_ref),
            (w_hbm, w_ref), (pairs_hbm, pairs_ref), (adj_hbm, adj_ref),
            (labs_hbm, labs_ref), (lab_hbm, lab_ref), (bias_hbm, bias_ref), (cross_hbm, cross_ref),
        ))
    ]
    for load in loads:
        load.start()
    for load in loads[:7]:
        load.wait()
    gain = down(gain_ref[...], S)
    shift = down(shift_ref[...], S)
    b1 = down(b1_ref[...], S)
    b2 = down(b2_ref[...], S)
    for t in range(2):
        v = x_ref[t].astype(F32)
        mean = jnp.mean(v, axis=0, keepdims=True)
        var = jnp.mean((v - mean) ** 2, axis=0, keepdims=True)
        n = ((v - mean) * lax.rsqrt(var + 1e-05) * gain + shift).astype(BF16)
        own[0, t * C:(t + 1) * C, :] = (
            jnp.dot(w1_ref[...], n, preferred_element_type=F32) + b1
        ).astype(BF16)
        own[1, t * C:(t + 1) * C, :] = (
            jnp.dot(w2_ref[...], n, preferred_element_type=F32) + b2
        ).astype(BF16)

    pl.semaphore_wait(barrier, NCOL - 1 + NY - 1 + NK * (NX - 1))

    def block(ref, index):
        return ref.at[pl.ds(pl.multiple_of(index * OWN, OWN), OWN), :]

    def arrived(ref, sem):
        pltpu.make_async_copy(ref, ref, sem).wait()

    def leg_y(d):
        return remote(own.at[1], ystage.at[y], y_send.at[d], y_recv.at[y],
                      lax.rem(y + d, NY) * NX + x, col)

    def leg_z(d):
        y2 = lax.rem(y + d, NY)
        return remote(ystage.at[y2], zstage.at[z], z_send.at[d], z_recv.at[z],
                      row, y2 * NK + k)

    def leg_x(d, dx):
        slot = lax.rem(z + d, NZ)
        b = (x % 2) * NCOL + slot * NK + k
        return remote(zstage.at[slot], block(rt, b), r_send.at[d, dx], r_recv.at[b],
                      y * NX + lax.rem(x + dx, NX), z * NK + home)

    def left(d):
        c2 = lax.rem(z + d, NZ) * NK + k if d else z * NK + 1 - k
        return remote(own.at[0], block(lt, col), l_send.at[d], l_recv.at[col], row, c2)

    def pass_on(d):
        c2 = lax.rem(z + d, NZ) * NK + k
        return remote(block(lt, c2), block(lt, c2), l_fwd.at[d], l_recv.at[c2],
                      row, z * NK + 1 - k)

    def turn_z(d):
        y2 = lax.rem(y + d, NY)
        if d:
            arrived(ystage.at[y2], y_recv.at[y2])

        @pl.when(y2 != z)
        def _():
            leg_z(d).start()

        @pl.when(y2 == z)
        def _():
            zstage[z] = ystage[z]

    def turn_x(d):
        slot = lax.rem(z + d, NZ)
        if d:
            arrived(zstage.at[slot], z_recv.at[slot])
        for dx in range(1, NX):
            leg_x(d, dx).start()

        @pl.when(home != k)
        def _():
            leg_x(d, 0).start()

        @pl.when(home == k)
        def _():
            b = (x % 2) * NCOL + slot * NK + k
            rt[pl.ds(pl.multiple_of(b * OWN, OWN), OWN), :] = zstage[slot]

    def share(d):
        c2 = lax.rem(z + d, NZ) * NK + k
        arrived(block(lt, c2), l_recv.at[c2])
        pass_on(d).start()

    for d in FAR:
        leg_y(d).start()
        left(d).start()
    left(0).start()
    ystage[y] = own[1]
    lt[pl.ds(pl.multiple_of(col * OWN, OWN), OWN), :] = own[0]
    turn_z(0)

    wide[...] = jnp.zeros_like(wide)
    loads[7].wait()
    wf[...] = w_ref[...].astype(F32)

    @pl.loop(0, C)
    def _(e):
        we = wf[pl.ds(e, C, stride=C), :].astype(BF16)
        for a in range(G):
            wide[pl.ds(pl.multiple_of(e * G * C + a * C, C), C), a * PW:(a + 1) * PW] = we

    for load in loads[8:]:
        load.wait()
    hits = jnp.int32(0)
    for n in range(pairs_ref.shape[1]):
        hits = hits + (pairs_ref[0, n] == y).astype(jnp.int32) * (
            pairs_ref[1, n] == z
        ).astype(jnp.int32)
    listed = hits.astype(F32)
    for i in range(TI):
        lhs[(i // G) * TJ:(i // G + 1) * TJ, (i % G) * PW:(i % G + 1) * PW] = (
            adj_ref[i].astype(F32) * listed
        ).astype(BF16)

    def outer_grad(first, last):
        @pl.loop(first, last)
        def _(n):
            part = lax.dot_general(
                lhs[...], wide[pl.ds(pl.multiple_of(n * 512, 512), 512), :],
                (((1,), (1,)), ((), ())), preferred_element_type=F32,
            ).astype(BF16)
            for q in range(4):
                for g in range(NG):
                    og[n * 4 + q, :, g * 128:(g + 1) * 128] = (
                        part[g * TJ:(g + 1) * TJ, q * 128:(q + 1) * 128]
                    )

    outer_grad(0, 8)
    for d in NEAR[1:]:
        turn_z(d)
    for d in NEAR[1:]:
        share(d)
    for zz in range(NZ):
        c2 = zz * NK + 1 - k
        arrived(block(lt, c2), l_recv.at[c2])

    def grad_x(y2, dx):
        x2 = lax.rem(x + dx, NX)
        return remote(rg.at[y2 * NX + x2], rx.at[dx - 1, y2], gx_send.at[dx - 1, y2],
                      gx_recv.at[dx - 1, y2], y * NX + x2, col)

    for n in range(TJ // JC):
        acc[...] = jnp.dot(
            og[:, n * JC:(n + 1) * JC, :].reshape(C * JC, TI * C), lt[...],
            preferred_element_type=F32,
        ) * (1.0 / S)
        for j in range(JC):
            at = n * JC + j
            rg[at // 2, (at % 2) * C:(at % 2 + 1) * C, :] = (
                acc[pl.ds(j, C, stride=JC), :].astype(BF16)
            )

    for d in NEAR:
        turn_x(d)
    for y2 in range(NY):
        for dx in range(1, NX):
            grad_x(y2, dx).start()

    left_t = lt[...].T
    for xx in range(2):
        for kk in range(NK):
            @pl.when(jnp.logical_or(2 * k + xx != x, kk != k))
            def _(xx=xx, kk=kk):
                for zz in range(NZ):
                    b = xx * NCOL + zz * NK + kk
                    arrived(block(rt, b), r_recv.at[b])

    for h in range(2):
        wf[...] = rt[h * TI * C:(h + 1) * TI * C, :].astype(F32)
        for e in range(C):
            rtp[e * TJ + h * TI:e * TJ + (h + 1) * TI, :] = (
                wf[pl.ds(e, TI, stride=C), :].astype(BF16)
            )

    right_t = rtp[...].T

    def grad_col(c2):
        return remote(lg.at[c2], lx.at[col], lg_send.at[c2], lg_recv.at[col], row, c2)

    for n in range(4):
        part = jnp.dot(
            right_t, og[:, :, n * 256:(n + 1) * 256].reshape(C * TJ, 256),
            preferred_element_type=F32,
        ) * (1.0 / S)
        lg[n * 4:(n + 1) * 4] = part.T.astype(BF16).reshape(4, OWN, S)
        for c2 in range(4 * n, 4 * n + 4):
            @pl.when(c2 != col)
            def _(c2=c2):
                grad_col(c2).start()

    def grad_y(y2):
        return remote(ys.at[y2], ry.at[y], gy_send.at[y2], gy_recv.at[y], y2 * NX + x, col)

    for y2 in range(NY):
        total = rg[y2 * NX + x].astype(F32)
        for dx in range(1, NX):
            grad_x(y2, dx).wait_recv()
            total = total + rx[dx - 1, y2].astype(F32)

        @pl.when(y2 != y)
        def _():
            ys[y2] = total.astype(BF16)
            grad_y(y2).start()

        @pl.when(y2 == y)
        def _():
            sums[1] = total

    @pl.loop(0, C // 4)
    def _(n):
        part = (jnp.dot(
            rtp[pl.ds(pl.multiple_of(n * 256, 256), 256), :], left_t, preferred_element_type=F32,
        ) * (1.0 / S)).astype(BF16)
        for q in range(4):
            for g in range(NG):
                fa[g * TJ:(g + 1) * TJ, pl.ds(pl.multiple_of((n * 4 + q) * 128, 128), 128)] = (
                    part[q * TJ:(q + 1) * TJ, g * 128:(g + 1) * 128]
                )

    labels = down(lab_ref[pl.ds(z, 1), :], PW)
    mine = jnp.where(k == 0, labels[:TJ], labels[TJ:])
    bias = bias_ref[...] * listed
    cross = cross_ref[...] * listed
    for h in range(2):
        part = jnp.dot(fa[...], wide[:, h * 256:(h + 1) * 256], preferred_element_type=F32)
        for g in range(NG):
            for a in range(2):
                i = g * G + h * 2 + a
                apart = (mine != labs_ref[row * TI + i]).astype(F32)
                pair[i] = (
                    part[g * TJ:(g + 1) * TJ, a * PW:(a + 1) * PW] * listed + bias + cross * apart
                ).astype(BF16)

    pair_copy = pltpu.make_async_copy(pair, out_hbm, out_sem.at[0])
    pair_copy.start()

    total = lg[col].astype(F32)
    for d in range(1, NCOL):
        c2 = lax.rem(col + d, NCOL)
        arrived(lx.at[c2], lg_recv.at[c2])
        total = total + lx[c2].astype(F32)
    sums[0] = total

    total = sums[1]
    for d in range(1, NY):
        y2 = lax.rem(y + d, NY)
        arrived(ry.at[y2], gy_recv.at[y2])
        total = total + ry[y2].astype(F32)
    sums[1] = total

    sums_copy = pltpu.make_async_copy(sums, grads_hbm, out_sem.at[1])
    sums_copy.start()

    for d in range(NY):
        left(d).wait_send()
        if d:
            leg_y(d).wait_send()
            pass_on(d).wait_send()
        for dx in range(1, NX):
            leg_x(d, dx).wait_send()
            grad_x(d, dx).wait_send()

        @pl.when(lax.rem(y + d, NY) != z)
        def _():
            leg_z(d).wait_send()

        @pl.when(home != k)
        def _():
            leg_x(d, 0).wait_send()

        @pl.when(d != y)
        def _():
            grad_y(d).wait_send()
    for c2 in range(NCOL):
        @pl.when(c2 != col)
        def _(c2=c2):
            grad_col(c2).wait_send()
    pair_copy.wait()
    sums_copy.wait()


def hand_over(pair_in, grads_in, pair_out, left_out, right_out, pair, grads, sems):
    rows = TI // 4
    moves = [(grads_in.at[n], grads.at[n], out) for n, out in enumerate((left_out, right_out))] + [
        (pair_in.at[part], pair.at[part], pair_out.at[part])
        for part in (pl.ds(n * rows, rows) for n in range(4))
    ]
    ins = [pltpu.make_async_copy(a, b, sems.at[0, n]) for n, (a, b, _) in enumerate(moves)]
    outs = [pltpu.make_async_copy(b, c, sems.at[1, n]) for n, (_, b, c) in enumerate(moves)]
    for copy in ins:
        copy.start()
    for first, then in zip(ins, outs):
        first.wait()
        then.start()
    for copy in outs:
        copy.wait()


def hbm():
    return pl.BlockSpec(memory_space=pltpu.HBM)


def per_device(
    sequence_features, standardize_scale, standardize_shift,
    first_projection_kernel, first_projection_shift,
    second_projection_kernel, second_projection_shift,
    final_projection_kernel, final_projection_shift, cross_molecule_shift,
    residue_molecule_label, selected_tile_couples, result_adjoint,
):
    dma = pltpu.SemaphoreType.DMA
    block = (OWN, S)
    pair, grads = pl.pallas_call(
        kernel,
        out_shape=(
            jax.ShapeDtypeStruct((TI, TJ, PW), BF16),
            jax.ShapeDtypeStruct((2, OWN, S), F32),
        ),
        in_specs=[hbm()] * 14,
        out_specs=(hbm(), hbm()),
        scratch_shapes=[
            pltpu.VMEM((2, FEATURES, S), BF16),
            pltpu.VMEM((1, FEATURES), F32),
            pltpu.VMEM((1, FEATURES), F32),
            pltpu.VMEM((C, FEATURES), BF16),
            pltpu.VMEM((1, C), F32),
            pltpu.VMEM((C, FEATURES), BF16),
            pltpu.VMEM((1, C), F32),
            pltpu.VMEM((C * C, PW), BF16),
            pltpu.SMEM((2, LISTED), jnp.int32),
            pltpu.VMEM((TI, TJ, PW), BF16),
            pltpu.SMEM((TOKENS,), jnp.int32),
            pltpu.VMEM((NZ, BLK), jnp.int32),
            pltpu.VMEM((1, PW), F32),
            pltpu.VMEM((1, PW), F32),
            pltpu.VMEM((2,) + block, BF16),
            pltpu.VMEM((NY,) + block, BF16),
            pltpu.VMEM((NZ,) + block, BF16),
            pltpu.VMEM((TI * C, S), BF16),
            pltpu.VMEM((TJ * C, S), BF16),
            pltpu.VMEM((C * G * C, G * PW), BF16),
            pltpu.VMEM((C * C, PW), F32),
            pltpu.VMEM((C * JC, S), F32),
            pltpu.VMEM((TJ * C, S), BF16),
            pltpu.VMEM((NG * TJ, G * PW), BF16),
            pltpu.VMEM((C, TJ, TI * C), BF16),
            pltpu.VMEM((NG * TJ, C * G * C), BF16),
            pltpu.VMEM((NCOL,) + block, BF16),
            pltpu.VMEM((NX * NY,) + block, BF16),
            pltpu.VMEM((NCOL,) + block, BF16),
            pltpu.VMEM((NX - 1, NY) + block, BF16),
            pltpu.VMEM((NY,) + block, BF16),
            pltpu.VMEM((NY,) + block, BF16),
            pltpu.VMEM((TI, TJ, PW), BF16),
            pltpu.VMEM((2,) + block, F32),
            dma((14,)), dma((2,)),
            dma((NZ,)), dma((NZ,)), dma((NCOL,)),
            dma((NY,)), dma((NY,)), dma((NY,)), dma((NZ,)),
            dma((NZ, NX)), dma((2 * NCOL,)),
            dma((NCOL,)), dma((NCOL,)),
            dma((NX - 1, NY)), dma((NX - 1, NY)),
            dma((NY,)), dma((NY,)),
        ],
        compiler_params=pltpu.CompilerParams(
            collective_id=0, has_side_effects=True, vmem_limit_bytes=60 * 2**20
        ),
        name="pair_block",
    )(
        sequence_features.transpose(1, 2, 0),
        standardize_scale[None], standardize_shift[None],
        first_projection_kernel.T, first_projection_shift[None],
        second_projection_kernel.T, second_projection_shift[None],
        final_projection_kernel, selected_tile_couples.T, result_adjoint,
        residue_molecule_label, residue_molecule_label.reshape(NZ, BLK),
        final_projection_shift[None], cross_molecule_shift[None],
    )

    pair, left, right = pl.pallas_call(
        hand_over,
        out_shape=(
            jax.ShapeDtypeStruct((TI, TJ, PW), BF16),
            jax.ShapeDtypeStruct(block, F32),
            jax.ShapeDtypeStruct(block, F32),
        ),
        in_specs=[hbm()] * 2,
        out_specs=(hbm(),) * 3,
        scratch_shapes=[
            pltpu.VMEM((TI, TJ, PW), BF16),
            pltpu.VMEM((2,) + block, F32),
            dma((2, 6)),
        ],
        compiler_params=pltpu.CompilerParams(vmem_limit_bytes=60 * 2**20),
        name="hand_over",
    )(pair, grads)

    def back(grad):
        return grad.reshape(2, C, S).transpose(2, 0, 1)

    return pair, back(left), back(right)


def solution(mesh):
    placed = (P(None, ("row", "col"), None),) + (P(),) * 11 + (P("row", "col", None),)
    return jax.shard_map(
        per_device,
        mesh=mesh,
        in_specs=placed,
        out_specs=(
            P("row", "col", None),
            P(None, ("row", "col"), None),
            P(None, ("col", "row"), None),
        ),
        check_vma=False,
    )
```

```python
import jax
import jax.numpy as jnp
from jax import lax
from jax.experimental import pallas as pl
from jax.experimental.pallas import tpu as pltpu
from jax.sharding import PartitionSpec as P

F32 = jnp.float32
BF16 = jnp.bfloat16
MESH = pl.DeviceIdType.MESH

NX, NY, NZ, NK = 4, 8, 8, 2
NCOL = NZ * NK
S = 128
C = 32
PW = 128
TI = 32
TJ = 64
OWN = 2 * C
G = 4
NG = TI // G
BLK = 128
FEATURES = 64
LISTED = 16
TOKENS = 1024


def place():
    row, col = lax.axis_index("row"), lax.axis_index("col")
    return row, col, row % NX, row // NX, col // NK, col % NK


def remote(src, dst, send, recv, row, col):
    return pltpu.make_async_remote_copy(
        src_ref=src, dst_ref=dst, send_sem=send, recv_sem=recv,
        device_id=(row, col), device_id_type=MESH,
    )


def down(vector, width):
    return jnp.broadcast_to(vector, (width, vector.shape[1])).T


NEAR = (0, 1, 7, 2, 6, 3, 5, 4)
FAR = (4, 3, 5, 2, 6, 1, 7)
JC = 16


def kernel(
    x_hbm, gain_hbm, shift_hbm, w1_hbm, b1_hbm, w2_hbm, b2_hbm,
    w_hbm, pairs_hbm, adj_hbm, labs_hbm, lab_hbm, bias_hbm, cross_hbm,
    out_hbm, grads_hbm,
    x_ref, gain_ref, shift_ref, w1_ref, b1_ref, w2_ref, b2_ref,
    w_ref, pairs_ref, adj_ref, labs_ref, lab_ref, bias_ref, cross_ref,
    own, ystage, zstage, lt, rt, wide, wf, acc, rtp, lhs, og, fa,
    lg, rg, lx, rx, ry, ys, pair, sums,
    in_sem, out_sem, l_send, l_fwd, l_recv, y_send, y_recv, z_send, z_recv, r_send, r_recv,
    lg_send, lg_recv, gx_send, gx_recv, gy_send, gy_recv,
):
    row, col, x, y, z, k = place()
    home = x // 2
    barrier = pltpu.get_barrier_semaphore()

    def greet(r, c):
        pl.semaphore_signal(barrier, inc=1, device_id=(r, c), device_id_type=MESH)

    for d in FAR:
        greet(lax.rem(y + d, NY) * NX + x, col)
        for kk in range(NK):
            greet(row, lax.rem(z + d, NZ) * NK + kk)
    greet(row, z * NK + 1 - k)
    for dx in range(1, NX):
        for kk in range(NK):
            greet(y * NX + lax.rem(x + dx, NX), z * NK + kk)

    loads = [
        pltpu.make_async_copy(src, dst, in_sem.at[n])
        for n, (src, dst) in enumerate((
            (x_hbm, x_ref), (gain_hbm, gain_ref), (shift_hbm, shift_ref),
            (w1_hbm, w1_ref), (b1_hbm, b1_ref), (w2_hbm, w2_ref), (b2_hbm, b2_ref),
            (w_hbm, w_ref), (pairs_hbm, pairs_ref), (adj_hbm, adj_ref),
            (labs_hbm, labs_ref), (lab_hbm, lab_ref), (bias_hbm, bias_ref), (cross_hbm, cross_ref),
        ))
    ]
    for load in loads:
        load.start()
    for load in loads[:7]:
        load.wait()
    gain = down(gain_ref[...], S)
    shift = down(shift_ref[...], S)
    b1 = down(b1_ref[...], S)
    b2 = down(b2_ref[...], S)
    for t in range(2):
        v = x_ref[t].astype(F32)
        mean = jnp.mean(v, axis=0, keepdims=True)
        var = jnp.mean((v - mean) ** 2, axis=0, keepdims=True)
        n = ((v - mean) * lax.rsqrt(var + 1e-05) * gain + shift).astype(BF16)
        own[0, t * C:(t + 1) * C, :] = (
            jnp.dot(w1_ref[...], n, preferred_element_type=F32) + b1
        ).astype(BF16)
        own[1, t * C:(t + 1) * C, :] = (
            jnp.dot(w2_ref[...], n, preferred_element_type=F32) + b2
        ).astype(BF16)

    pl.semaphore_wait(barrier, NCOL - 1 + NY - 1 + NK * (NX - 1))

    def block(ref, index):
        return ref.at[pl.ds(pl.multiple_of(index * OWN, OWN), OWN), :]

    def arrived(ref, sem):
        pltpu.make_async_copy(ref, ref, sem).wait()

    def leg_y(d):
        return remote(own.at[1], ystage.at[y], y_send.at[d], y_recv.at[y],
                      lax.rem(y + d, NY) * NX + x, col)

    def leg_z(d):
        y2 = lax.rem(y + d, NY)
        return remote(ystage.at[y2], zstage.at[z], z_send.at[d], z_recv.at[z],
                      row, y2 * NK + k)

    def leg_x(d, dx):
        slot = lax.rem(z + d, NZ)
        b = (x % 2) * NCOL + slot * NK + k
        return remote(zstage.at[slot], block(rt, b), r_send.at[d, dx], r_recv.at[b],
                      y * NX + lax.rem(x + dx, NX), z * NK + home)

    def left(d):
        c2 = lax.rem(z + d, NZ) * NK + k if d else z * NK + 1 - k
        return remote(own.at[0], block(lt, col), l_send.at[d], l_recv.at[col], row, c2)

    def pass_on(d):
        c2 = lax.rem(z + d, NZ) * NK + k
        return remote(block(lt, c2), block(lt, c2), l_fwd.at[d], l_recv.at[c2],
                      row, z * NK + 1 - k)

    def turn_z(d):
        y2 = lax.rem(y + d, NY)
        if d:
            arrived(ystage.at[y2], y_recv.at[y2])

        @pl.when(y2 != z)
        def _():
            leg_z(d).start()

        @pl.when(y2 == z)
        def _():
            zstage[z] = ystage[z]

    def turn_x(d):
        slot = lax.rem(z + d, NZ)
        if d:
            arrived(zstage.at[slot], z_recv.at[slot])
        for dx in range(1, NX):
            leg_x(d, dx).start()

        @pl.when(home != k)
        def _():
            leg_x(d, 0).start()

        @pl.when(home == k)
        def _():
            b = (x % 2) * NCOL + slot * NK + k
            rt[pl.ds(pl.multiple_of(b * OWN, OWN), OWN), :] = zstage[slot]

    def share(d):
        c2 = lax.rem(z + d, NZ) * NK + k
        arrived(block(lt, c2), l_recv.at[c2])
        pass_on(d).start()

    for d in FAR:
        leg_y(d).start()
        left(d).start()
    left(0).start()
    ystage[y] = own[1]
    lt[pl.ds(pl.multiple_of(col * OWN, OWN), OWN), :] = own[0]
    turn_z(0)

    wide[...] = jnp.zeros_like(wide)
    loads[7].wait()
    wf[...] = w_ref[...].astype(F32)

    @pl.loop(0, C)
    def _(e):
        we = wf[pl.ds(e, C, stride=C), :].astype(BF16)
        for a in range(G):
            wide[pl.ds(pl.multiple_of(e * G * C + a * C, C), C), a * PW:(a + 1) * PW] = we

    for load in loads[8:]:
        load.wait()
    hits = jnp.int32(0)
    for n in range(pairs_ref.shape[1]):
        hits = hits + (pairs_ref[0, n] == y).astype(jnp.int32) * (
            pairs_ref[1, n] == z
        ).astype(jnp.int32)
    listed = hits.astype(F32)
    for i in range(TI):
        lhs[(i // G) * TJ:(i // G + 1) * TJ, (i % G) * PW:(i % G + 1) * PW] = (
            adj_ref[i].astype(F32) * listed
        ).astype(BF16)

    def outer_grad(first, last):
        @pl.loop(first, last)
        def _(n):
            part = lax.dot_general(
                lhs[...], wide[pl.ds(pl.multiple_of(n * 512, 512), 512), :],
                (((1,), (1,)), ((), ())), preferred_element_type=F32,
            ).astype(BF16)
            for q in range(4):
                for g in range(NG):
                    og[n * 4 + q, :, g * 128:(g + 1) * 128] = (
                        part[g * TJ:(g + 1) * TJ, q * 128:(q + 1) * 128]
                    )

    for d in NEAR[1:]:
        turn_z(d)
    for d in NEAR[1:]:
        share(d)
    outer_grad(0, 8)
    for zz in range(NZ):
        c2 = zz * NK + 1 - k
        arrived(block(lt, c2), l_recv.at[c2])

    def grad_x(y2, dx):
        x2 = lax.rem(x + dx, NX)
        return remote(rg.at[y2 * NX + x2], rx.at[dx - 1, y2], gx_send.at[dx - 1, y2],
                      gx_recv.at[dx - 1, y2], y * NX + x2, col)

    for n in range(TJ // JC):
        acc[...] = jnp.dot(
            og[:, n * JC:(n + 1) * JC, :].reshape(C * JC, TI * C), lt[...],
            preferred_element_type=F32,
        ) * (1.0 / S)
        for j in range(JC):
            at = n * JC + j
            rg[at // 2, (at % 2) * C:(at % 2 + 1) * C, :] = (
                acc[pl.ds(j, C, stride=JC), :].astype(BF16)
            )

    for d in NEAR:
        turn_x(d)
    for y2 in range(NY):
        for dx in range(1, NX):
            grad_x(y2, dx).start()

    left_t = lt[...].T
    for xx in range(2):
        for kk in range(NK):
            @pl.when(jnp.logical_or(2 * k + xx != x, kk != k))
            def _(xx=xx, kk=kk):
                for zz in range(NZ):
                    b = xx * NCOL + zz * NK + kk
                    arrived(block(rt, b), r_recv.at[b])

    for h in range(2):
        wf[...] = rt[h * TI * C:(h + 1) * TI * C, :].astype(F32)
        for e in range(C):
            rtp[e * TJ + h * TI:e * TJ + (h + 1) * TI, :] = (
                wf[pl.ds(e, TI, stride=C), :].astype(BF16)
            )

    right_t = rtp[...].T

    def grad_col(c2):
        return remote(lg.at[c2], lx.at[col], lg_send.at[c2], lg_recv.at[col], row, c2)

    for n in range(4):
        part = jnp.dot(
            right_t, og[:, :, n * 256:(n + 1) * 256].reshape(C * TJ, 256),
            preferred_element_type=F32,
        ) * (1.0 / S)
        lg[n * 4:(n + 1) * 4] = part.T.astype(BF16).reshape(4, OWN, S)
        for c2 in range(4 * n, 4 * n + 4):
            @pl.when(c2 != col)
            def _(c2=c2):
                grad_col(c2).start()

    def grad_y(y2):
        return remote(ys.at[y2], ry.at[y], gy_send.at[y2], gy_recv.at[y], y2 * NX + x, col)

    for y2 in range(NY):
        total = rg[y2 * NX + x].astype(F32)
        for dx in range(1, NX):
            grad_x(y2, dx).wait_recv()
            total = total + rx[dx - 1, y2].astype(F32)

        @pl.when(y2 != y)
        def _():
            ys[y2] = total.astype(BF16)
            grad_y(y2).start()

        @pl.when(y2 == y)
        def _():
            sums[1] = total

    @pl.loop(0, C // 4)
    def _(n):
        part = (jnp.dot(
            rtp[pl.ds(pl.multiple_of(n * 256, 256), 256), :], left_t, preferred_element_type=F32,
        ) * (1.0 / S)).astype(BF16)
        for q in range(4):
            for g in range(NG):
                fa[g * TJ:(g + 1) * TJ, pl.ds(pl.multiple_of((n * 4 + q) * 128, 128), 128)] = (
                    part[q * TJ:(q + 1) * TJ, g * 128:(g + 1) * 128]
                )

    labels = down(lab_ref[pl.ds(z, 1), :], PW)
    mine = jnp.where(k == 0, labels[:TJ], labels[TJ:])
    bias = bias_ref[...] * listed
    cross = cross_ref[...] * listed
    for h in range(2):
        part = jnp.dot(fa[...], wide[:, h * 256:(h + 1) * 256], preferred_element_type=F32)
        for g in range(NG):
            for a in range(2):
                i = g * G + h * 2 + a
                apart = (mine != labs_ref[row * TI + i]).astype(F32)
                pair[i] = (
                    part[g * TJ:(g + 1) * TJ, a * PW:(a + 1) * PW] * listed + bias + cross * apart
                ).astype(BF16)

    pair_copy = pltpu.make_async_copy(pair, out_hbm, out_sem.at[0])
    pair_copy.start()

    total = lg[col].astype(F32)
    for d in range(1, NCOL):
        c2 = lax.rem(col + d, NCOL)
        arrived(lx.at[c2], lg_recv.at[c2])
        total = total + lx[c2].astype(F32)
    sums[0] = total

    total = sums[1]
    for d in range(1, NY):
        y2 = lax.rem(y + d, NY)
        arrived(ry.at[y2], gy_recv.at[y2])
        total = total + ry[y2].astype(F32)
    sums[1] = total

    sums_copy = pltpu.make_async_copy(sums, grads_hbm, out_sem.at[1])
    sums_copy.start()

    for d in range(NY):
        left(d).wait_send()
        if d:
            leg_y(d).wait_send()
            pass_on(d).wait_send()
        for dx in range(1, NX):
            leg_x(d, dx).wait_send()
            grad_x(d, dx).wait_send()

        @pl.when(lax.rem(y + d, NY) != z)
        def _():
            leg_z(d).wait_send()

        @pl.when(home != k)
        def _():
            leg_x(d, 0).wait_send()

        @pl.when(d != y)
        def _():
            grad_y(d).wait_send()
    for c2 in range(NCOL):
        @pl.when(c2 != col)
        def _(c2=c2):
            grad_col(c2).wait_send()
    pair_copy.wait()
    sums_copy.wait()


def hand_over(pair_in, grads_in, pair_out, left_out, right_out, pair, grads, sems):
    rows = TI // 4
    moves = [(grads_in.at[n], grads.at[n], out) for n, out in enumerate((left_out, right_out))] + [
        (pair_in.at[part], pair.at[part], pair_out.at[part])
        for part in (pl.ds(n * rows, rows) for n in range(4))
    ]
    ins = [pltpu.make_async_copy(a, b, sems.at[0, n]) for n, (a, b, _) in enumerate(moves)]
    outs = [pltpu.make_async_copy(b, c, sems.at[1, n]) for n, (_, b, c) in enumerate(moves)]
    for copy in ins:
        copy.start()
    for first, then in zip(ins, outs):
        first.wait()
        then.start()
    for copy in outs:
        copy.wait()


def hbm():
    return pl.BlockSpec(memory_space=pltpu.HBM)


def per_device(
    sequence_features, standardize_scale, standardize_shift,
    first_projection_kernel, first_projection_shift,
    second_projection_kernel, second_projection_shift,
    final_projection_kernel, final_projection_shift, cross_molecule_shift,
    residue_molecule_label, selected_tile_couples, result_adjoint,
):
    dma = pltpu.SemaphoreType.DMA
    block = (OWN, S)
    pair, grads = pl.pallas_call(
        kernel,
        out_shape=(
            jax.ShapeDtypeStruct((TI, TJ, PW), BF16),
            jax.ShapeDtypeStruct((2, OWN, S), F32),
        ),
        in_specs=[hbm()] * 14,
        out_specs=(hbm(), hbm()),
        scratch_shapes=[
            pltpu.VMEM((2, FEATURES, S), BF16),
            pltpu.VMEM((1, FEATURES), F32),
            pltpu.VMEM((1, FEATURES), F32),
            pltpu.VMEM((C, FEATURES), BF16),
            pltpu.VMEM((1, C), F32),
            pltpu.VMEM((C, FEATURES), BF16),
            pltpu.VMEM((1, C), F32),
            pltpu.VMEM((C * C, PW), BF16),
            pltpu.SMEM((2, LISTED), jnp.int32),
            pltpu.VMEM((TI, TJ, PW), BF16),
            pltpu.SMEM((TOKENS,), jnp.int32),
            pltpu.VMEM((NZ, BLK), jnp.int32),
            pltpu.VMEM((1, PW), F32),
            pltpu.VMEM((1, PW), F32),
            pltpu.VMEM((2,) + block, BF16),
            pltpu.VMEM((NY,) + block, BF16),
            pltpu.VMEM((NZ,) + block, BF16),
            pltpu.VMEM((TI * C, S), BF16),
            pltpu.VMEM((TJ * C, S), BF16),
            pltpu.VMEM((C * G * C, G * PW), BF16),
            pltpu.VMEM((C * C, PW), F32),
            pltpu.VMEM((C * JC, S), F32),
            pltpu.VMEM((TJ * C, S), BF16),
            pltpu.VMEM((NG * TJ, G * PW), BF16),
            pltpu.VMEM((C, TJ, TI * C), BF16),
            pltpu.VMEM((NG * TJ, C * G * C), BF16),
            pltpu.VMEM((NCOL,) + block, BF16),
            pltpu.VMEM((NX * NY,) + block, BF16),
            pltpu.VMEM((NCOL,) + block, BF16),
            pltpu.VMEM((NX - 1, NY) + block, BF16),
            pltpu.VMEM((NY,) + block, BF16),
            pltpu.VMEM((NY,) + block, BF16),
            pltpu.VMEM((TI, TJ, PW), BF16),
            pltpu.VMEM((2,) + block, F32),
            dma((14,)), dma((2,)),
            dma((NZ,)), dma((NZ,)), dma((NCOL,)),
            dma((NY,)), dma((NY,)), dma((NY,)), dma((NZ,)),
            dma((NZ, NX)), dma((2 * NCOL,)),
            dma((NCOL,)), dma((NCOL,)),
            dma((NX - 1, NY)), dma((NX - 1, NY)),
            dma((NY,)), dma((NY,)),
        ],
        compiler_params=pltpu.CompilerParams(
            collective_id=0, has_side_effects=True, vmem_limit_bytes=60 * 2**20
        ),
        name="pair_block",
    )(
        sequence_features.transpose(1, 2, 0),
        standardize_scale[None], standardize_shift[None],
        first_projection_kernel.T, first_projection_shift[None],
        second_projection_kernel.T, second_projection_shift[None],
        final_projection_kernel, selected_tile_couples.T, result_adjoint,
        residue_molecule_label, residue_molecule_label.reshape(NZ, BLK),
        final_projection_shift[None], cross_molecule_shift[None],
    )

    pair, left, right = pl.pallas_call(
        hand_over,
        out_shape=(
            jax.ShapeDtypeStruct((TI, TJ, PW), BF16),
            jax.ShapeDtypeStruct(block, F32),
            jax.ShapeDtypeStruct(block, F32),
        ),
        in_specs=[hbm()] * 2,
        out_specs=(hbm(),) * 3,
        scratch_shapes=[
            pltpu.VMEM((TI, TJ, PW), BF16),
            pltpu.VMEM((2,) + block, F32),
            dma((2, 6)),
        ],
        compiler_params=pltpu.CompilerParams(vmem_limit_bytes=60 * 2**20),
        name="hand_over",
    )(pair, grads)

    def back(grad):
        return grad.reshape(2, C, S).transpose(2, 0, 1)

    return pair, back(left), back(right)


def solution(mesh):
    placed = (P(None, ("row", "col"), None),) + (P(),) * 11 + (P("row", "col", None),)
    return jax.shard_map(
        per_device,
        mesh=mesh,
        in_specs=placed,
        out_specs=(
            P("row", "col", None),
            P(None, ("row", "col"), None),
            P(None, ("col", "row"), None),
        ),
        check_vma=False,
    )
```
